512 devices in a mesh: seq: 16 (over z), exp: 32 (over x, y, core).
Axes of the slice: x: 4, y: 4, z: 16, core: 2. Of those that a mesh axis runs over, the one named last changes fastest.
Arguments:
- patches: bfloat16 [32, 3584, 3072], P('exp', 'seq'), may hold values from -8 to 8
- slot_keys: bfloat16 [32, 3072], P('exp'), may hold values from -0.05593081 to 0.05593081
- w_in: bfloat16 [32, 3072, 3072], P('exp', None, 'seq'), may hold values from -0.109375 to 0.109375
- w_out: bfloat16 [32, 3072, 3072], P('exp', 'seq'), may hold values from -0.21875 to 0.21875
Outputs:
- mixed: bfloat16 [32, 3584, 3072], P('exp', 'seq')
The draws below stay inside these ranges and needn't reach their ends.
All inputs are finite; a program needn't handle non-finite values.
Results may differ from the reference program's by a relative error of at most 0.0071.
Values may be sent and summed in bfloat16 or wider, within the bound.
No kernel may reach another device: no remote copies, remote signals or barrier semaphores. Data moves between devices by JAX's collectives and lax.ppermute only.
A program may use at most 64 MiB of HBM per device.

```python
import jax
import jax.numpy as jnp
from jax import lax

D = 3072
FFN = 3072
EXPERTS = 32
IMAGES = 32
PATCHES = 3584


key_spread = 2.5


def key_table(key):
    sign_key, size_key = jax.random.split(key)
    signs = jnp.where(jax.random.bernoulli(sign_key, 0.5, (EXPERTS, D)), 1.0, -1.0)
    sizes = jax.random.uniform(size_key, (EXPERTS, D), jnp.float32, 0.8, 1.2)
    return signs * sizes * (key_spread * D ** (-0.5))


def draw_slot_keys(key, part):
    table = key_table(key)
    return table.astype(jnp.bfloat16)


def draw_patches(key, part):
    key = jax.random.fold_in(key, 5)
    base_key = jax.random.fold_in(key, 0)
    values = jnp.clip(jax.random.normal(base_key, (IMAGES, PATCHES, D), jnp.float32), -6.0, 6.0)
    return values.astype(jnp.bfloat16)


def block_scale(stream_key, shape, cuts, least, top_value):
    gain = 1.0
    for dim, parts in cuts:
        steps = jax.random.uniform(jax.random.fold_in(jax.random.fold_in(stream_key, 6), dim), (parts,), jnp.float32, least / len(cuts), top_value / len(cuts))
        gain = gain * jnp.repeat(jnp.exp(steps), shape[dim] // parts).reshape((-1,) + (1,) * (len(shape) - 1 - dim))
    return gain


def bell_draw(key, dims, width, bound, cuts=(), kind=jnp.bfloat16):
    values = width * jax.random.normal(key, dims, jnp.float32)
    if cuts:
        values = values * block_scale(key, dims, cuts, -0.22, 0.18)
    return jnp.clip(values, -bound, bound).astype(kind)


def setup_inputs(seed: int = 0) -> dict:
    arg_keys = jax.random.split(jax.random.key(seed), 5)
    return {
        "patches": draw_patches(jax.random.fold_in(arg_keys[4], 71), 0),
        "slot_keys": draw_slot_keys(jax.random.fold_in(arg_keys[4], 71), 0),
        "w_in": bell_draw(arg_keys[2], (EXPERTS, D, FFN), D ** -0.5, 0.109375, ((0, 32), (2, 16))),
        "w_out": bell_draw(arg_keys[3], (EXPERTS, FFN, D), (FFN // 4) ** -0.5, 0.21875, ((0, 32), (1, 16))),
    }


def per_image(image_rows, slot_keys):
    logits = jnp.dot(image_rows, slot_keys.T, preferred_element_type=jnp.float32)
    column_max = jnp.max(logits, axis=0)
    raised = jnp.exp(logits - column_max[None, :])
    dispatch = raised.astype(jnp.bfloat16)
    denom = jnp.sum(raised, axis=0)
    slot_sum = jnp.dot(dispatch.T, image_rows, preferred_element_type=jnp.float32)
    slot_in = (slot_sum / denom[:, None]).astype(jnp.bfloat16)
    combine = jax.nn.softmax(logits, axis=1).astype(jnp.bfloat16)
    return slot_in, combine


def per_expert(operands):
    slot_rows, first, second = operands
    hidden = jnp.dot(slot_rows, first, preferred_element_type=jnp.float32)
    activated = jax.nn.gelu(hidden).astype(jnp.bfloat16)
    return jnp.dot(activated, second, preferred_element_type=jnp.float32).astype(jnp.bfloat16)


def mix_image(operands):
    combine, outputs = operands
    return jnp.dot(combine, outputs, preferred_element_type=jnp.float32).astype(jnp.bfloat16)


def reference(patches, slot_keys, w_in, w_out):
    slot_in, combine = lax.map(lambda rows: per_image(rows, slot_keys), patches)
    slot_out = lax.map(per_expert, (jnp.transpose(slot_in, (1, 0, 2)), w_in, w_out))
    return lax.map(mix_image, (combine, jnp.transpose(slot_out, (1, 0, 2))))
```

```python
import functools

import jax
import jax.numpy as jnp
from jax import lax
from jax.experimental import pallas as pl
from jax.experimental.pallas import tpu as pltpu
from jax.sharding import PartitionSpec as P

F32 = jnp.float32
BF16 = jnp.bfloat16
SEQ = 16
EXP = 32
LANES = 128
D = 3072
BLOCKS = D // LANES
HALF = LANES // 2
FULL = 32
PACKED = 48
STATS = 56
SMALL = 16

VMEM = pl.BlockSpec(memory_space=pltpu.VMEM)


def call(kernel, outs, scratch=(), n_in=1, flops=0, n_bytes=0):
    return pl.pallas_call(
        kernel,
        out_shape=outs,
        in_specs=[VMEM] * n_in,
        out_specs=jax.tree.map(lambda _: VMEM, outs),
        scratch_shapes=list(scratch),
        cost_estimate=pl.CostEstimate(flops=flops, bytes_accessed=n_bytes, transcendentals=0),
        compiler_params=pltpu.CompilerParams(vmem_limit_bytes=24 * 1024 * 1024),
    )


def left_lanes(rows):
    return lax.broadcasted_iota(jnp.int32, (rows, LANES), 1) < HALF


def swap(x):
    return pltpu.roll(x, HALF, 1)


def pack_halves(block):
    top, low = block[:16], block[16:]
    left = left_lanes(16)
    return jnp.where(left, top, swap(low)), jnp.where(left, swap(top), low)


def unpack_halves(even, odd):
    left = left_lanes(16)
    top = jnp.where(left, even, swap(odd))
    low = jnp.where(left, swap(even), odd)
    return jnp.concatenate([top, low], axis=0)


def store_shares(out_ref, term, base):
    for k in range(term.shape[1] // LANES):
        block = base // LANES + k
        piece = term[:, k * LANES : (k + 1) * LANES]
        if block < SEQ:
            out_ref[block, 0:FULL, :] = piece.astype(BF16)
        else:
            even, odd = pack_halves(piece)
            share = 2 * (block - SEQ)
            out_ref[share, FULL:PACKED, :] = even.astype(BF16)
            out_ref[share + 1, FULL:PACKED, :] = odd.astype(BF16)


def load_shares(in_ref, rows_ref):
    for block in range(SEQ):
        rows_ref[:, block * LANES : (block + 1) * LANES] = in_ref[block, 0:FULL, :]
    for j in range(BLOCKS - SEQ):
        even = in_ref[2 * j, FULL:PACKED, :].astype(F32)
        odd = in_ref[2 * j + 1, FULL:PACKED, :].astype(F32)
        block = SEQ + j
        rows_ref[:, block * LANES : (block + 1) * LANES] = unpack_halves(even, odd).astype(BF16)


def dispatch_kernel(patch_ref, keys_ref, out_ref, logits_ref, spread_ref, table_ref):
    spread_ref[...] = keys_ref[...].astype(F32).reshape(EXP * BLOCKS, LANES)
    for k in range(BLOCKS):
        rows = spread_ref[pl.ds(k, EXP, stride=BLOCKS), :]
        table_ref[:, k * LANES : (k + 1) * LANES] = rows.astype(BF16)
    logits = lax.dot_general(
        table_ref[...], patch_ref[...], (((1,), (1,)), ((), ())), preferred_element_type=F32
    )
    logits_ref[...] = logits
    shift = jnp.max(logits, axis=1, keepdims=True).astype(BF16).astype(F32)
    raised = jnp.exp(logits - shift)
    denom = jnp.sum(raised, axis=1, keepdims=True)
    weights = raised.astype(BF16)
    high = denom.astype(BF16).astype(F32)
    low = denom - high
    row = lax.broadcasted_iota(jnp.int32, (EXP, LANES), 0)
    lane = lax.broadcasted_iota(jnp.int32, (EXP, LANES), 1)
    spots = jnp.where(lane == row, shift, 0.0)
    spots += jnp.where(lane == row + EXP, high, 0.0)
    spots += jnp.where(lane == row + 2 * EXP, low, 0.0)
    stats = jnp.broadcast_to(jnp.sum(spots, axis=0, keepdims=True), (STATS - PACKED, LANES)).astype(BF16)
    for share in range(SEQ):
        out_ref[share, PACKED:STATS, :] = stats
    step = 512
    for base in range(0, D, step):
        term = jnp.dot(weights, patch_ref[:, base : base + step], preferred_element_type=F32)
        store_shares(out_ref, term, base)


def store_small(out_ref, full, half):
    half = jnp.concatenate([half, swap(half)], axis=0)
    row = lax.broadcasted_iota(jnp.int32, (SMALL, LANES), 0)
    for e in range(EXP):
        whole = jnp.broadcast_to(full[e : e + 1], (SMALL, LANES))
        part = jnp.broadcast_to(half[e : e + 1], (SMALL, LANES))
        out_ref[e] = jnp.where(row == 0, whole, part).astype(BF16)


def merge_kernel(in_ref, out_ref):
    stats = jnp.concatenate([in_ref[s, PACKED:STATS, :].astype(F32)[0:1] for s in range(SEQ)], axis=0)
    shift = stats
    high = pltpu.roll(stats, LANES - EXP, 1)
    low = pltpu.roll(stats, LANES - 2 * EXP, 1)
    lane = lax.broadcasted_iota(jnp.int32, (SEQ, LANES), 1)
    scale = jnp.exp(shift - jnp.max(shift, axis=0, keepdims=True))
    denom = jnp.sum(scale * (high + low), axis=0, keepdims=True)
    scale = jnp.where(lane < EXP, scale / denom, 0.0)
    scale = jnp.concatenate([scale, jnp.zeros((LANES - SEQ, LANES), F32)], axis=0)
    columns = scale.T
    full = jnp.zeros((FULL, LANES), F32)
    half = jnp.zeros((16, LANES), F32)
    left = left_lanes(16)
    for s in range(SEQ):
        factor = columns[0:EXP, s : s + 1]
        full += factor * in_ref[s, 0:FULL, :].astype(F32)
        packed = jnp.where(left, factor[:16], factor[16:])
        half += packed * in_ref[s, FULL:PACKED, :].astype(F32)
    store_small(out_ref, full, half)


def add_kernel(in_ref, out_ref):
    full = jnp.zeros((FULL, LANES), F32)
    half = jnp.zeros((16, LANES), F32)
    for s in range(SEQ):
        full += in_ref[s, 0:FULL, :].astype(F32)
        half += in_ref[s, FULL:PACKED, :].astype(F32)
    store_small(out_ref, full, half)


def gather_kernel(in_ref, out_ref, spread_ref):
    spread_ref[...] = in_ref[...].astype(F32).reshape(EXP * SMALL, LANES)
    full = spread_ref[pl.ds(0, EXP, stride=SMALL), :].astype(BF16)
    half = spread_ref[pl.ds(1, EXP, stride=SMALL), :]
    half = jnp.where(left_lanes(16), half[:16], swap(half[16:])).astype(BF16)
    for s in range(SEQ):
        out_ref[s, 0:FULL, :] = full
        out_ref[s, FULL:PACKED, :] = half


def ffn_kernel(in_ref, first_ref, second_ref, out_ref, rows_ref):
    load_shares(in_ref, rows_ref)
    hidden = jnp.dot(rows_ref[...], first_ref[...], preferred_element_type=F32)
    activated = jax.nn.gelu(hidden).astype(BF16)
    step = 512
    for base in range(0, D, step):
        term = jnp.dot(activated, second_ref[:, base : base + step], preferred_element_type=F32)
        store_shares(out_ref, term, base)


def mix_kernel(in_ref, logits_ref, out_ref, rows_ref, combine_ref, *, step):
    @pl.when(pl.program_id(0) == 0)
    def _():
        load_shares(in_ref, rows_ref)
        logits = logits_ref[...]
        raised = jnp.exp(logits - jnp.max(logits, axis=0, keepdims=True))
        combine = raised / jnp.sum(raised, axis=0, keepdims=True)
        combine_ref[...] = combine.T.astype(BF16)

    base = pl.multiple_of(pl.program_id(0) * step, step)
    out_ref[...] = jnp.dot(
        combine_ref[...], rows_ref[:, pl.ds(base, step)], preferred_element_type=F32
    ).astype(BF16)


def exchange(x, axis):
    return lax.all_to_all(x, axis, split_axis=0, concat_axis=0, tiled=True)


def shards(patches, slot_keys, w_in, w_out):
    patch_rows = patches[0]
    rows = patch_rows.shape[0]
    sds = jax.ShapeDtypeStruct
    own_key = jnp.broadcast_to(slot_keys.reshape(1, BLOCKS, LANES), (EXP, BLOCKS, LANES))
    keys = exchange(own_key, "exp")
    terms, logits = call(
        dispatch_kernel,
        (sds((SEQ, STATS, LANES), BF16), sds((EXP, rows), F32)),
        [pltpu.VMEM((EXP * BLOCKS, LANES), F32), pltpu.VMEM((EXP, D), BF16)],
        n_in=2,
    )(patch_rows, keys)
    small = sds((EXP, SMALL, LANES), BF16)
    shares = sds((SEQ, PACKED, LANES), BF16)
    spread = [pltpu.VMEM((EXP * SMALL, LANES), F32)]
    slot_part = call(merge_kernel, small)(exchange(terms, "seq"))
    slot_shares = call(gather_kernel, shares, spread)(exchange(slot_part, "exp"))
    out_terms = call(ffn_kernel, shares, [pltpu.VMEM((EXP, D), BF16)], n_in=3)(
        exchange(slot_shares, "seq"), w_in[0], w_out[0]
    )
    out_part = call(add_kernel, small)(exchange(out_terms, "seq"))
    out_shares = call(gather_kernel, shares, spread)(exchange(out_part, "exp"))
    step = 768
    mixed = pl.pallas_call(
        functools.partial(mix_kernel, step=step),
        grid=(D // step,),
        out_shape=sds((rows, D), BF16),
        in_specs=[VMEM, VMEM],
        out_specs=pl.BlockSpec((rows, step), lambda j: (0, j)),
        scratch_shapes=[pltpu.VMEM((EXP, D), BF16), pltpu.VMEM((rows, EXP), BF16)],
        compiler_params=pltpu.CompilerParams(vmem_limit_bytes=24 * 1024 * 1024),
    )(exchange(out_shares, "seq"), logits)
    return mixed[None]


def solution(mesh):
    placed = (P("exp", "seq", None), P("exp", None), P("exp", None, "seq"), P("exp", "seq", None))
    return jax.shard_map(
        shards, mesh=mesh, in_specs=placed, out_specs=P("exp", "seq", None), check_vma=False
    )
```

```python
import jax
import jax.numpy as jnp
from jax import lax
from jax.experimental import pallas as pl
from jax.experimental.pallas import tpu as pltpu
from jax.sharding import Mesh, PartitionSpec as P

F32 = jnp.float32
BF16 = jnp.bfloat16
SEQ = 16
EXP = 32
SIDE = 4
PEERS = SEQ * SIDE
LANES = 128
D = 3072
BLOCKS = D // LANES
HALF = LANES // 2
ROWS = 16
VMEM = pl.BlockSpec(memory_space=pltpu.VMEM)
HBM = pl.BlockSpec(memory_space=pltpu.HBM)
SMEM = pl.BlockSpec(memory_space=pltpu.SMEM)
LIMIT = 24 * 1024 * 1024
sds = jax.ShapeDtypeStruct


def call(kernel, outs, in_specs, scratch=(), out_specs=None, flops=0, n_bytes=0):
    return pl.pallas_call(
        kernel,
        out_shape=outs,
        in_specs=in_specs,
        out_specs=jax.tree.map(lambda _: VMEM, outs) if out_specs is None else out_specs,
        scratch_shapes=list(scratch),
        cost_estimate=pl.CostEstimate(flops=flops, bytes_accessed=n_bytes, transcendentals=0),
        compiler_params=pltpu.CompilerParams(vmem_limit_bytes=LIMIT),
    )


def lanes_left():
    return lax.broadcasted_iota(jnp.int32, (8, LANES), 1) < HALF


def rows_top():
    return lax.broadcasted_iota(jnp.int32, (8, LANES), 0) < 4


def swap(x):
    return pltpu.roll(x, HALF, 1)


def turn(x):
    return pltpu.roll(x, 4, 0)


def store_shares(out_ref, term_ref, stats):
    left, top = lanes_left(), rows_top()

    def pair(j, _):
        low = pl.multiple_of(2 * j * LANES, 2 * LANES)
        high = pl.multiple_of((SEQ + j) * LANES, LANES)
        for g in range(SIDE):
            rows = slice(8 * g, 8 * g + 8)
            whole = term_ref[rows, pl.ds(low, 2 * LANES)]
            part = term_ref[rows, pl.ds(high, LANES)]
            other = turn(part)
            even = jnp.where(left, part, swap(other))
            odd = jnp.where(left, swap(part), other)
            if stats is not None:
                even = jnp.where(top, even, stats[g])
                odd = jnp.where(top, odd, stats[g])
            first = jnp.concatenate([whole[:, :LANES], even], axis=0)
            second = jnp.concatenate([whole[:, LANES:], odd], axis=0)
            out_ref[2 * SIDE * j + g] = first.astype(BF16)
            out_ref[2 * SIDE * j + SIDE + g] = second.astype(BF16)
        return 0

    lax.fori_loop(0, SEQ // 2, pair, 0)


def load_shares(in_ref, rows_ref):
    left, top = lanes_left(), rows_top()

    def pair(j, _):
        firsts, seconds, parts = [], [], []
        for g in range(SIDE):
            first = in_ref[2 * SIDE * j + g].astype(F32)
            second = in_ref[2 * SIDE * j + SIDE + g].astype(F32)
            firsts.append(first[:8])
            seconds.append(second[:8])
            even, odd = first[8:], second[8:]
            upper = jnp.where(left, even, swap(odd))
            lower = jnp.where(left, swap(even), odd)
            parts.append(jnp.where(top, upper, turn(lower)))
        low = pl.multiple_of(2 * j * LANES, 2 * LANES)
        high = pl.multiple_of((SEQ + j) * LANES, LANES)
        rows_ref[:, pl.ds(low, LANES)] = jnp.concatenate(firsts, axis=0).astype(BF16)
        rows_ref[:, pl.ds(low + LANES, LANES)] = jnp.concatenate(seconds, axis=0).astype(BF16)
        rows_ref[:, pl.ds(high, LANES)] = jnp.concatenate(parts, axis=0).astype(BF16)
        return 0

    lax.fori_loop(0, SEQ // 2, pair, 0)


def load_kernel(src_ref, out_ref, sem):
    copy = pltpu.make_async_copy(src_ref, out_ref, sem)
    copy.start()
    copy.wait()


def dispatch_kernel(place_ref, patch_ref, keys_ref, out_ref, logits_ref, spread_ref, table_ref, term_ref):
    spread_ref[...] = keys_ref[...].astype(F32).reshape(EXP * BLOCKS, LANES)
    for k in range(BLOCKS):
        rows = spread_ref[pl.ds(k, EXP, stride=BLOCKS), :]
        table_ref[:, k * LANES : (k + 1) * LANES] = rows.astype(BF16)
    logits = lax.dot_general(
        table_ref[...], patch_ref[...], (((1,), (1,)), ((), ())), preferred_element_type=F32
    )
    logits_ref[...] = logits
    shift = jnp.max(logits, axis=1, keepdims=True).astype(BF16).astype(F32)
    raised = jnp.exp(logits - shift)
    denom = jnp.sum(raised, axis=1, keepdims=True)
    weights = raised.astype(BF16)
    high = denom.astype(BF16).astype(F32)
    low = denom - high
    place = place_ref[0]
    lane = lax.broadcasted_iota(jnp.int32, (EXP, LANES), 1)
    spots = jnp.where(lane == place, shift, 0.0)
    spots += jnp.where(lane == place + SEQ, high, 0.0)
    spots += jnp.where(lane == place + 2 * SEQ, low, 0.0)
    stats = []
    for g in range(SIDE):
        tile = spots[8 * g : 8 * g + 8]
        stats.append(turn(tile) + swap(tile))
    for base in range(0, D, 768):
        term_ref[:, base : base + 768] = jnp.dot(
            weights, patch_ref[:, base : base + 768], preferred_element_type=F32
        )
    store_shares(out_ref, term_ref, stats)


def store_cores(out_ref, wholes, halves):
    top = rows_top()
    spread = [jnp.where(top, h, turn(swap(h))) for h in halves]
    low, high = [], []
    for tiles in (wholes, spread):
        for a, b in ((0, 1), (2, 3)):
            low.append(jnp.where(top, tiles[a], turn(tiles[b])))
            high.append(jnp.where(top, turn(tiles[a]), tiles[b]))
    out_ref[0] = jnp.concatenate(low, axis=0).astype(BF16)
    out_ref[1] = jnp.concatenate(high, axis=0).astype(BF16)


def merge_kernel(in_ref, out_ref):
    left, top = lanes_left(), rows_top()
    gathered = []
    for g in range(SIDE):
        total = in_ref[g, :, :].astype(F32)[8:]
        for s in range(1, SEQ):
            total += in_ref[SIDE * s + g, :, :].astype(F32)[8:]
        gathered.append(jnp.where(top, turn(total), swap(total)))
    stats = jnp.concatenate(gathered, axis=0)
    valid = lax.broadcasted_iota(jnp.int32, (EXP, LANES), 1) < SEQ
    largest = jnp.max(jnp.where(valid, stats, -jnp.inf), axis=1, keepdims=True)
    scale = jnp.exp(jnp.where(valid, stats - largest, 0.0))
    denoms = pltpu.roll(stats, LANES - SEQ, 1) + pltpu.roll(stats, LANES - 2 * SEQ, 1)
    denom = jnp.sum(jnp.where(valid, scale * denoms, 0.0), axis=1, keepdims=True)
    scale = scale / denom
    wholes, halves = [], []
    for g in range(SIDE):
        whole = jnp.zeros((8, LANES), F32)
        half = jnp.zeros((8, LANES), F32)
        for s in range(SEQ):
            factor = jnp.broadcast_to(scale[8 * g : 8 * g + 8, s : s + 1], (8, LANES))
            block = in_ref[SIDE * s + g].astype(F32)
            whole += factor * block[:8]
            half += jnp.where(left, factor, turn(factor)) * block[8:]
        wholes.append(whole)
        halves.append(half)
    store_cores(out_ref, wholes, halves)


def add_kernel(in_ref, out_ref):
    wholes, halves = [], []
    for g in range(SIDE):
        total = in_ref[g].astype(F32)
        for s in range(1, SEQ):
            total += in_ref[SIDE * s + g].astype(F32)
        wholes.append(total[:8])
        halves.append(total[8:])
    store_cores(out_ref, wholes, halves)


def regroup_kernel(in_ref, out_ref, spread_ref):
    left = lanes_left()
    for c in range(2):
        both = in_ref[c].astype(F32)
        spread_ref[16 * c : 16 * c + 16, :] = both[:16]
        spread_ref[32 + 16 * c : 48 + 16 * c, :] = both[16:]
    for g in range(SIDE):
        whole = spread_ref[pl.ds(g, 8, stride=SIDE), :]
        half = spread_ref[pl.ds(32 + g, 8, stride=SIDE), :]
        half = jnp.where(left, half, swap(turn(half)))
        block = jnp.concatenate([whole, half], axis=0).astype(BF16)
        for s in range(SEQ):
            out_ref[SIDE * s + g] = block


def ffn_kernel(in_ref, first_ref, second_ref, out_ref, rows_ref, term_ref):
    load_shares(in_ref, rows_ref)
    hidden = lax.dot_general(
        rows_ref[...], first_ref[...], (((1,), (1,)), ((), ())), preferred_element_type=F32
    )
    activated = jax.nn.gelu(hidden).astype(BF16)
    for base in range(0, D, 768):
        term_ref[:, base : base + 768] = jnp.dot(
            activated, second_ref[:, base : base + 768], preferred_element_type=F32
        )
    store_shares(out_ref, term_ref, None)


def combine_kernel(logits_ref, out_ref):
    logits = logits_ref[...]
    raised = jnp.exp(logits - jnp.max(logits, axis=0, keepdims=True))
    combine = raised / jnp.sum(raised, axis=0, keepdims=True)
    out_ref[...] = combine.T.astype(BF16)


def mix_kernel(in_ref, combine_ref, out_ref, rows_ref, mixed_ref, sems):
    load_shares(in_ref, rows_ref)
    copies = []
    step = D // len(MIX_STEPS)
    for j in MIX_STEPS:
        cols = slice(j * step, (j + 1) * step)
        mixed_ref[:, cols] = jnp.dot(
            combine_ref[...], rows_ref[:, cols], preferred_element_type=F32
        ).astype(BF16)
        copies.append(pltpu.make_async_copy(mixed_ref.at[:, cols], out_ref.at[:, cols], sems.at[j]))
        copies[-1].start()
    for copy in copies:
        copy.wait()


MIX_STEPS = range(6)


def exchange(x, axes):
    return lax.all_to_all(x, axes, split_axis=0, concat_axis=0, tiled=True)


def shards(patches, slot_keys, w_in, w_out):
    rows = patches.shape[1]
    wide = sds((PEERS, ROWS, LANES), BF16)
    small = sds((2, 2 * ROWS, LANES), BF16)
    table = pltpu.VMEM((EXP, D), BF16)
    term = pltpu.VMEM((EXP, D), F32)

    own_key = jnp.broadcast_to(slot_keys.reshape(1, BLOCKS, LANES), (EXP, BLOCKS, LANES))
    keys = exchange(own_key, ("x", "core", "y"))
    patch_rows = call(
        load_kernel, sds((rows, D), BF16), [HBM], [pltpu.SemaphoreType.DMA], n_bytes=4 * rows * D
    )(patches[0])
    place = lax.axis_index("seq").astype(jnp.int32).reshape(1)
    terms, logits = call(
        dispatch_kernel,
        (wide, sds((EXP, rows), F32)),
        [SMEM, VMEM, VMEM],
        [pltpu.VMEM((EXP * BLOCKS, LANES), F32), table, term],
    )(place, patch_rows, keys)
    combine = call(combine_kernel, sds((rows, EXP), BF16), [VMEM], n_bytes=1 << 20)(logits)

    spread = [pltpu.VMEM((64, LANES), F32)]
    slot_part = call(merge_kernel, small, [VMEM])(exchange(terms, ("seq", "x")))
    slot_tiles = call(regroup_kernel, wide, [VMEM], spread)(exchange(slot_part, "core"))
    out_terms = call(ffn_kernel, wide, [VMEM] * 3, [table, term])(
        exchange(slot_tiles, ("seq", "y")), w_in[0].T, w_out[0]
    )
    out_part = call(add_kernel, small, [VMEM])(exchange(out_terms, ("seq", "y")))
    out_tiles = call(regroup_kernel, wide, [VMEM], spread)(exchange(out_part, "core"))
    mixed = call(
        mix_kernel,
        sds((rows, D), BF16),
        [VMEM, VMEM],
        [table, pltpu.VMEM((rows, D), BF16), pltpu.SemaphoreType.DMA((len(MIX_STEPS),))],
        out_specs=HBM,
    )(exchange(out_tiles, ("seq", "x")), combine)
    return mixed[None]


def solution(mesh):
    split = Mesh(mesh.devices.reshape(SEQ, SIDE, SIDE, 2), ("seq", "x", "y", "core"))
    exp = ("x", "y", "core")
    placed = (P(exp, "seq", None), P(exp, None), P(exp, None, "seq"), P(exp, "seq", None))
    return jax.shard_map(
        shards, mesh=split, in_specs=placed, out_specs=P(exp, "seq", None), check_vma=False
    )
```

```python
import jax
import jax.numpy as jnp
from jax import lax
from jax.experimental import pallas as pl
from jax.experimental.pallas import tpu as pltpu
from jax.sharding import Mesh, PartitionSpec as P

F32 = jnp.float32
BF16 = jnp.bfloat16
SIDE = 4
CORES = 2
EXP = SIDE * SIDE * CORES
LANES = 128
D = 3072
BLOCKS = D // LANES
SHARE = BLOCKS // SIDE
PAIRS = SHARE // 2
PEERS = SIDE * SIDE
WIDE = 8 * SHARE
NARROW = 16 * SHARE
VMEM = pl.BlockSpec(memory_space=pltpu.VMEM)
SMEM = pl.BlockSpec(memory_space=pltpu.SMEM)
ANY = pl.BlockSpec(memory_space=pl.ANY)
LIMIT = 24 * 1024 * 1024
sds = jax.ShapeDtypeStruct


def call(kernel, outs, in_specs, scratch=(), out_specs=None):
    return pl.pallas_call(
        kernel,
        out_shape=outs,
        in_specs=in_specs,
        out_specs=jax.tree.map(lambda _: VMEM, outs) if out_specs is None else out_specs,
        scratch_shapes=list(scratch),
        compiler_params=pltpu.CompilerParams(vmem_limit_bytes=LIMIT),
    )


def rows_top():
    return lax.broadcasted_iota(jnp.int32, (8, LANES), 0) < 4


def swap(x):
    return pltpu.roll(x, LANES // 2, 1)


def turn(x):
    return pltpu.roll(x, 4, 0)


def store_share(out_ref, z, term):
    for g in range(SIDE):
        tiles = term[8 * g : 8 * g + 8]
        for m in range(PAIRS):
            low = tiles[:, 2 * m * LANES : (2 * m + 1) * LANES]
            high = tiles[:, (2 * m + 1) * LANES : (2 * m + 2) * LANES]
            pair = jnp.concatenate([low, high], axis=0).astype(BF16)
            out_ref[SIDE * z + g, 16 * m : 16 * m + 16, :] = pair


def load_share(in_ref, z):
    columns = []
    for m in range(PAIRS):
        pairs = [in_ref[SIDE * z + g, 16 * m : 16 * m + 16, :].astype(F32) for g in range(SIDE)]
        columns.append(jnp.concatenate([p[:8] for p in pairs], axis=0))
        columns.append(jnp.concatenate([p[8:] for p in pairs], axis=0))
    return jnp.concatenate(columns, axis=1).astype(BF16)


def spread_stats(place, shift, denom):
    lane = lax.broadcasted_iota(jnp.int32, (shift.shape[0], LANES), 1)
    high = denom.astype(BF16).astype(F32)
    stats = jnp.where(lane == place, shift, 0.0)
    stats = jnp.where(lane == place + SIDE, high, stats)
    return jnp.where(lane == place + 2 * SIDE, denom - high, stats)


def merge_stats(stats):
    valid = lax.broadcasted_iota(jnp.int32, stats.shape, 1) < SIDE
    largest = jnp.max(jnp.where(valid, stats, -jnp.inf), axis=1, keepdims=True)
    scale = jnp.exp(jnp.where(valid, stats - largest, 0.0))
    parts = pltpu.roll(stats, LANES - SIDE, 1) + pltpu.roll(stats, LANES - 2 * SIDE, 1)
    denom = jnp.sum(jnp.where(valid, scale * parts, 0.0), axis=1, keepdims=True)
    return largest, scale, denom


def dispatch_kernel(place_ref, patch_ref, keys_ref, out_ref, combine_ref, spread_ref, table_ref):
    spread_ref[...] = keys_ref[...].astype(F32).reshape(EXP * BLOCKS, LANES)
    for k in range(BLOCKS):
        rows = spread_ref[pl.ds(k, EXP, stride=BLOCKS), :]
        table_ref[:, k * LANES : (k + 1) * LANES] = rows.astype(BF16)
    logits = lax.dot_general(
        table_ref[...], patch_ref[0], (((1,), (1,)), ((), ())), preferred_element_type=F32
    )
    shift = jnp.max(logits, axis=1, keepdims=True).astype(BF16).astype(F32)
    raised = jnp.exp(logits - shift)
    denom = jnp.sum(raised, axis=1, keepdims=True)
    weights = raised.astype(BF16)
    stats = spread_stats(place_ref[0], shift, denom).astype(BF16)
    for z in range(SIDE):
        base = z * SHARE * LANES
        columns = patch_ref[0, :, base : base + SHARE * LANES]
        store_share(out_ref, z, jnp.dot(weights, columns, preferred_element_type=F32))
        for g in range(SIDE):
            out_ref[SIDE * z + g, WIDE : WIDE + 8, :] = stats[8 * g : 8 * g + 8]
    raised = jnp.exp(logits - jnp.max(logits, axis=0, keepdims=True))
    combine = raised / jnp.sum(raised, axis=0, keepdims=True)
    combine_ref[...] = combine.T.astype(BF16)


def store_cores(out_ref, row, tiles):
    top = rows_top()
    low = [jnp.where(top, tiles[a], turn(tiles[a + 1])) for a in (0, 2)]
    high = [jnp.where(top, turn(tiles[a]), tiles[a + 1]) for a in (0, 2)]
    out_ref[0, row : row + 16, :] = jnp.concatenate(low, axis=0).astype(BF16)
    out_ref[1, row : row + 16, :] = jnp.concatenate(high, axis=0).astype(BF16)


def copy_cores(out_ref):
    for h in range(1, SIDE):
        for c in range(CORES):
            out_ref[CORES * h + c] = out_ref[c]


def sum_near(in_ref, out_ref, factor):
    for m in range(PAIRS):
        lows, highs = [], []
        for g in range(SIDE):
            low = high = None
            for z in range(SIDE):
                pair = in_ref[SIDE * z + g, 16 * m : 16 * m + 16, :].astype(F32)
                a, b = pair[:8], pair[8:]
                if factor is not None:
                    a, b = factor[g][z] * a, factor[g][z] * b
                low, high = (a, b) if z == 0 else (low + a, high + b)
            lows.append(low)
            highs.append(high)
        store_cores(out_ref, 32 * m, lows)
        store_cores(out_ref, 32 * m + 16, highs)


def merge_near_kernel(place_ref, in_ref, out_ref):
    gathered = []
    for g in range(SIDE):
        total = in_ref[g, WIDE : WIDE + 8, :].astype(F32)
        for z in range(1, SIDE):
            total += in_ref[SIDE * z + g, WIDE : WIDE + 8, :].astype(F32)
        gathered.append(total)
    largest, scale, denom = merge_stats(jnp.concatenate(gathered, axis=0))
    factor = [
        [jnp.broadcast_to(scale[8 * g : 8 * g + 8, z : z + 1], (8, LANES)) for z in range(SIDE)]
        for g in range(SIDE)
    ]
    sum_near(in_ref, out_ref, factor)
    stats = spread_stats(place_ref[0], largest, denom)
    top = rows_top()
    t = [stats[8 * g : 8 * g + 8] for g in range(SIDE)]
    low = jnp.where(top, t[0], turn(t[1])) + swap(jnp.where(top, t[2], turn(t[3])))
    high = jnp.where(top, turn(t[0]), t[1]) + swap(jnp.where(top, turn(t[2]), t[3]))
    out_ref[0, NARROW : NARROW + 8, :] = low.astype(BF16)
    out_ref[1, NARROW : NARROW + 8, :] = high.astype(BF16)
    copy_cores(out_ref)


def add_near_kernel(in_ref, out_ref):
    sum_near(in_ref, out_ref, None)
    copy_cores(out_ref)


def sum_far(in_ref, out_ref, spread_ref, factor):
    for k in range(SHARE):
        for c in range(CORES):
            total = None
            for h in range(SIDE):
                rows = in_ref[CORES * h + c, 16 * k : 16 * k + 16, :].astype(F32)
                if factor is not None:
                    rows = factor[c][h] * rows
                total = rows if h == 0 else total + rows
            spread_ref[32 * k + 16 * c : 32 * k + 16 * c + 16, :] = total
    for g in range(SIDE):
        for m in range(PAIRS):
            low = spread_ref[pl.ds(64 * m + g, 8, stride=SIDE), :]
            high = spread_ref[pl.ds(64 * m + 32 + g, 8, stride=SIDE), :]
            pair = jnp.concatenate([low, high], axis=0).astype(BF16)
            for z in range(SIDE):
                out_ref[SIDE * z + g, 16 * m : 16 * m + 16, :] = pair


def merge_far_kernel(in_ref, out_ref, spread_ref):
    gathered = []
    for c in range(CORES):
        total = in_ref[c, NARROW : NARROW + 8, :].astype(F32)
        for h in range(1, SIDE):
            total += in_ref[CORES * h + c, NARROW : NARROW + 8, :].astype(F32)
        gathered += [total, swap(total)]
    _, scale, denom = merge_stats(jnp.concatenate(gathered, axis=0))
    scale = scale / denom
    factor = [
        [jnp.broadcast_to(scale[16 * c : 16 * c + 16, h : h + 1], (16, LANES)) for h in range(SIDE)]
        for c in range(CORES)
    ]
    sum_far(in_ref, out_ref, spread_ref, factor)


def add_far_kernel(in_ref, out_ref, spread_ref):
    sum_far(in_ref, out_ref, spread_ref, None)


def ffn_kernel(in_ref, first_ref, second_ref, out_ref):
    hidden = None
    for z in range(SIDE):
        base = z * SHARE * LANES
        term = lax.dot_general(
            load_share(in_ref, z),
            first_ref[0, :, base : base + SHARE * LANES],
            (((1,), (1,)), ((), ())),
            preferred_element_type=F32,
        )
        hidden = term if z == 0 else hidden + term
    activated = jax.nn.gelu(hidden).astype(BF16)
    for z in range(SIDE):
        base = z * SHARE * LANES
        columns = second_ref[0, :, base : base + SHARE * LANES]
        store_share(out_ref, z, jnp.dot(activated, columns, preferred_element_type=F32))


def mix_kernel(in_ref, combine_ref, out_ref, mixed_ref, sems):
    copies = []
    for z in range(SIDE):
        columns = slice(z * SHARE * LANES, (z + 1) * SHARE * LANES)
        mixed_ref[:, columns] = jnp.dot(
            combine_ref[...], load_share(in_ref, z), preferred_element_type=F32
        ).astype(BF16)
        copy = pltpu.make_async_copy(mixed_ref.at[:, columns], out_ref.at[0, :, columns], sems.at[z])
        copy.start()
        copies.append(copy)
    for copy in copies:
        copy.wait()


def exchange(x, *axes):
    return lax.all_to_all(x, axes, split_axis=0, concat_axis=0, tiled=True)


def shards(patches, slot_keys, w_in, w_out):
    rows = patches.shape[1]
    wide = sds((PEERS, WIDE, LANES), BF16)
    narrow = sds((SIDE * CORES, NARROW, LANES), BF16)
    wide_stats = sds((PEERS, WIDE + 8, LANES), BF16)
    narrow_stats = sds((SIDE * CORES, NARROW + 8, LANES), BF16)
    place_near = lax.axis_index("zl").astype(jnp.int32).reshape(1)
    place_far = lax.axis_index("zh").astype(jnp.int32).reshape(1)

    own_key = jnp.broadcast_to(slot_keys.reshape(1, BLOCKS, LANES), (EXP, BLOCKS, LANES))
    own_key, place_near, place_far = lax.optimization_barrier((own_key, place_near, place_far))
    keys = exchange(own_key, "x", "core", "y")
    terms, combine = call(
        dispatch_kernel,
        (wide_stats, sds((rows, EXP), BF16)),
        [SMEM, VMEM, VMEM],
        [pltpu.VMEM((EXP * BLOCKS, LANES), F32), pltpu.VMEM((EXP, D), BF16)],
    )(place_near, patches, keys)

    spread = [pltpu.VMEM((32 * SHARE, LANES), F32)]
    near = call(merge_near_kernel, narrow_stats, [SMEM, VMEM])(place_far, exchange(terms, "zl", "x"))
    slot_tiles = call(merge_far_kernel, wide, [VMEM], spread)(exchange(near, "zh", "core"))
    out_terms = call(ffn_kernel, wide, [VMEM] * 3)(
        exchange(slot_tiles, "zl", "y"), jnp.swapaxes(w_in, 1, 2), w_out
    )
    near = call(add_near_kernel, narrow, [VMEM])(exchange(out_terms, "zl", "y"))
    out_tiles = call(add_far_kernel, wide, [VMEM], spread)(exchange(near, "zh", "core"))
    return call(
        mix_kernel,
        sds((1, rows, D), BF16),
        [VMEM, VMEM],
        [pltpu.VMEM((rows, D), BF16), pltpu.SemaphoreType.DMA((SIDE,))],
        out_specs=ANY,
    )(exchange(out_tiles, "zl", "x"), combine)


def solution(mesh):
    split = Mesh(
        mesh.devices.reshape(SIDE, SIDE, SIDE, SIDE, CORES), ("zh", "zl", "x", "y", "core")
    )
    seq, exp = ("zh", "zl"), ("x", "y", "core")
    placed = (P(exp, seq, None), P(exp, None), P(exp, None, seq), P(exp, seq, None))
    return jax.shard_map(
        shards, mesh=split, in_specs=placed, out_specs=P(exp, seq, None), check_vma=False
    )
```

```python
import jax
import jax.numpy as jnp
from jax import lax
from jax.experimental import pallas as pl
from jax.experimental.pallas import tpu as pltpu
from jax.sharding import Mesh, PartitionSpec as P

F32 = jnp.float32
BF16 = jnp.bfloat16
SIDE = 4
CORES = 2
EXP = SIDE * SIDE * CORES
LANES = 128
D = 3072
BLOCKS = D // LANES
SHARE = BLOCKS // SIDE
PAIRS = SHARE // 2
PEERS = SIDE * SIDE
TALL = 16 * SHARE
WIDE = 8 * SHARE
VMEM = pl.BlockSpec(memory_space=pltpu.VMEM)
SMEM = pl.BlockSpec(memory_space=pltpu.SMEM)
ANY = pl.BlockSpec(memory_space=pl.ANY)
LIMIT = 24 * 1024 * 1024
sds = jax.ShapeDtypeStruct


def call(kernel, outs, in_specs, scratch=(), out_specs=None):
    return pl.pallas_call(
        kernel,
        out_shape=outs,
        in_specs=in_specs,
        out_specs=jax.tree.map(lambda _: VMEM, outs) if out_specs is None else out_specs,
        scratch_shapes=list(scratch),
        compiler_params=pltpu.CompilerParams(vmem_limit_bytes=LIMIT),
    )


def rows_top():
    return lax.broadcasted_iota(jnp.int32, (8, LANES), 0) < 4


def swap(x):
    return pltpu.roll(x, LANES // 2, 1)


def turn(x):
    return pltpu.roll(x, 4, 0)


def split_cores(tiles):
    top = rows_top()
    low = [jnp.where(top, tiles[a], turn(tiles[a + 1])) for a in (0, 2)]
    high = [jnp.where(top, turn(tiles[a]), tiles[a + 1]) for a in (0, 2)]
    return jnp.concatenate(low, axis=0), jnp.concatenate(high, axis=0)


def pick(g, low, high):
    a, b = (rows[8 * (g // 2) : 8 * (g // 2) + 8] for rows in (low, high))
    return jnp.where(rows_top(), a, turn(b)) if g % 2 == 0 else jnp.where(rows_top(), turn(a), b)


def store_share(out_ref, z, term):
    for c in range(CORES):
        for k in range(SHARE):
            piece = term[16 * c : 16 * c + 16, k * LANES : (k + 1) * LANES]
            out_ref[CORES * z + c, 16 * k : 16 * k + 16, :] = piece.astype(BF16)


def load_share(in_ref, z):
    columns = []
    for m in range(PAIRS):
        pairs = [in_ref[SIDE * g + z, 16 * m : 16 * m + 16, :].astype(F32) for g in range(SIDE)]
        columns.append(jnp.concatenate(split_cores([p[:8] for p in pairs]), axis=0))
        columns.append(jnp.concatenate(split_cores([p[8:] for p in pairs]), axis=0))
    return jnp.concatenate(columns, axis=1).astype(BF16)


def spread_stats(place, shift, denom):
    lane = lax.broadcasted_iota(jnp.int32, (shift.shape[0], LANES), 1)
    high = denom.astype(BF16).astype(F32)
    stats = jnp.where(lane == place, shift, 0.0)
    stats = jnp.where(lane == place + SIDE, high, stats)
    return jnp.where(lane == place + 2 * SIDE, denom - high, stats)


def merge_stats(stats):
    valid = lax.broadcasted_iota(jnp.int32, stats.shape, 1) < SIDE
    largest = jnp.max(jnp.where(valid, stats, -jnp.inf), axis=1, keepdims=True)
    scale = jnp.exp(jnp.where(valid, stats - largest, 0.0))
    parts = pltpu.roll(stats, LANES - SIDE, 1) + pltpu.roll(stats, LANES - 2 * SIDE, 1)
    denom = jnp.sum(jnp.where(valid, scale * parts, 0.0), axis=1, keepdims=True)
    return largest, scale, denom


def key_kernel(key_ref, patch_ref, out_ref, spread_ref):
    del patch_ref
    for k in range(BLOCKS):
        spread_ref[k : k + 1, :] = key_ref[:, k * LANES : (k + 1) * LANES].astype(F32)
    block = spread_ref[...].astype(BF16)
    for e in range(EXP):
        out_ref[e] = block


def dispatch_kernel(place_ref, patch_ref, keys_ref, out_ref, combine_ref, spread_ref, table_ref):
    spread_ref[...] = keys_ref[...].astype(F32).reshape(EXP * BLOCKS, LANES)
    for k in range(BLOCKS):
        for c in range(CORES):
            rows = spread_ref[pl.ds(BLOCKS * c + k, 16, stride=CORES * BLOCKS), :]
            table_ref[16 * c : 16 * c + 16, k * LANES : (k + 1) * LANES] = rows.astype(BF16)
    logits = lax.dot_general(
        table_ref[...], patch_ref[0], (((1,), (1,)), ((), ())), preferred_element_type=F32
    )
    shift = jnp.max(logits, axis=1, keepdims=True).astype(BF16).astype(F32)
    raised = jnp.exp(logits - shift)
    denom = jnp.sum(raised, axis=1, keepdims=True)
    weights = raised.astype(BF16)
    rest = (raised - weights.astype(F32)).astype(BF16)
    weights = jnp.concatenate([weights, rest], axis=0)
    stats = spread_stats(place_ref[0], shift, denom)
    for z in range(SIDE):
        base = z * SHARE * LANES
        columns = patch_ref[0, :, base : base + SHARE * LANES]
        term = jnp.dot(weights, columns, preferred_element_type=F32)
        store_share(out_ref, z, term[:EXP] + term[EXP:])
        for c in range(CORES):
            both = stats[16 * c : 16 * c + 8] + swap(stats[16 * c + 8 : 16 * c + 16])
            out_ref[CORES * z + c, TALL : TALL + 8, :] = both.astype(BF16)
    raised = jnp.exp(logits - jnp.max(logits, axis=0, keepdims=True))
    combine = raised / jnp.sum(raised, axis=0, keepdims=True)
    combine_ref[...] = combine.T.astype(BF16)


def sum_near(in_ref, out_ref, factor):
    for m in range(PAIRS):
        sums = []
        for k in (2 * m, 2 * m + 1):
            for c in range(CORES):
                total = None
                for z in range(SIDE):
                    rows = in_ref[CORES * z + c, 16 * k : 16 * k + 16, :].astype(F32)
                    if factor is not None:
                        rows = factor[c][z] * rows
                    total = rows if z == 0 else total + rows
                sums.append(total)
        for g in range(SIDE):
            pair = [pick(g, sums[0], sums[1]), pick(g, sums[2], sums[3])]
            pair = jnp.concatenate(pair, axis=0).astype(BF16)
            for h in range(SIDE):
                out_ref[SIDE * g + h, 16 * m : 16 * m + 16, :] = pair


def merge_near_kernel(place_ref, in_ref, out_ref):
    gathered = []
    for c in range(CORES):
        total = in_ref[c, TALL : TALL + 8, :].astype(F32)
        for z in range(1, SIDE):
            total += in_ref[CORES * z + c, TALL : TALL + 8, :].astype(F32)
        gathered += [total, swap(total)]
    largest, scale, denom = merge_stats(jnp.concatenate(gathered, axis=0))
    factor = [
        [jnp.broadcast_to(scale[16 * c : 16 * c + 16, z : z + 1], (16, LANES)) for z in range(SIDE)]
        for c in range(CORES)
    ]
    sum_near(in_ref, out_ref, factor)
    stats = spread_stats(place_ref[0], largest, denom)
    for g in range(SIDE):
        tile = pick(g, stats[:16], stats[16:]).astype(BF16)
        for h in range(SIDE):
            out_ref[SIDE * g + h, WIDE : WIDE + 8, :] = tile


def add_near_kernel(in_ref, out_ref):
    sum_near(in_ref, out_ref, None)


def sum_far(in_ref, out_ref, spread_ref, factor):
    for m in range(PAIRS):
        lows, highs = [], []
        for g in range(SIDE):
            low = high = None
            for h in range(SIDE):
                pair = in_ref[SIDE * g + h, 16 * m : 16 * m + 16, :].astype(F32)
                a, b = pair[:8], pair[8:]
                if factor is not None:
                    a, b = factor[g][h] * a, factor[g][h] * b
                low, high = (a, b) if h == 0 else (low + a, high + b)
            lows.append(low)
            highs.append(high)
        spread_ref[64 * m : 64 * m + 32, :] = jnp.concatenate(split_cores(lows), axis=0)
        spread_ref[64 * m + 32 : 64 * m + 64, :] = jnp.concatenate(split_cores(highs), axis=0)
    for g in range(SIDE):
        for m in range(PAIRS):
            low = spread_ref[pl.ds(64 * m + g, 8, stride=SIDE), :]
            high = spread_ref[pl.ds(64 * m + 32 + g, 8, stride=SIDE), :]
            pair = jnp.concatenate([low, high], axis=0).astype(BF16)
            for z in range(SIDE):
                out_ref[SIDE * g + z, 16 * m : 16 * m + 16, :] = pair


def merge_far_kernel(in_ref, out_ref, spread_ref):
    gathered = []
    for g in range(SIDE):
        total = in_ref[SIDE * g, WIDE : WIDE + 8, :].astype(F32)
        for h in range(1, SIDE):
            total += in_ref[SIDE * g + h, WIDE : WIDE + 8, :].astype(F32)
        gathered.append(total)
    _, scale, denom = merge_stats(jnp.concatenate(gathered, axis=0))
    scale = scale / denom
    factor = [
        [jnp.broadcast_to(scale[8 * g : 8 * g + 8, h : h + 1], (8, LANES)) for h in range(SIDE)]
        for g in range(SIDE)
    ]
    sum_far(in_ref, out_ref, spread_ref, factor)


def add_far_kernel(in_ref, out_ref, spread_ref):
    sum_far(in_ref, out_ref, spread_ref, None)


def ffn_kernel(in_ref, first_ref, second_ref, out_ref):
    hidden = None
    for z in range(SIDE):
        base = z * SHARE * LANES
        term = lax.dot_general(
            load_share(in_ref, z),
            first_ref[0, :, base : base + SHARE * LANES],
            (((1,), (1,)), ((), ())),
            preferred_element_type=F32,
        )
        hidden = term if z == 0 else hidden + term
    activated = jax.nn.gelu(hidden).astype(BF16)
    for z in range(SIDE):
        base = z * SHARE * LANES
        columns = second_ref[0, :, base : base + SHARE * LANES]
        store_share(out_ref, z, jnp.dot(activated, columns, preferred_element_type=F32))


def mix_kernel(in_ref, combine_ref, out_ref, mixed_ref, sems):
    copies = []
    for z in range(SIDE):
        columns = slice(z * SHARE * LANES, (z + 1) * SHARE * LANES)
        mixed_ref[:, columns] = jnp.dot(
            combine_ref[...], load_share(in_ref, z), preferred_element_type=F32
        ).astype(BF16)
        copy = pltpu.make_async_copy(mixed_ref.at[:, columns], out_ref.at[0, :, columns], sems.at[z])
        copy.start()
        copies.append(copy)
    for copy in copies:
        copy.wait()


def exchange(x, *axes):
    return lax.all_to_all(x, axes, split_axis=0, concat_axis=0, tiled=True)


def shards(patches, slot_keys, w_in, w_out):
    rows = patches.shape[1]
    tall = sds((CORES * SIDE, TALL, LANES), BF16)
    tall_stats = sds((CORES * SIDE, TALL + 8, LANES), BF16)
    wide = sds((PEERS, WIDE, LANES), BF16)
    wide_stats = sds((PEERS, WIDE + 8, LANES), BF16)
    place_near = lax.axis_index("zl").astype(jnp.int32).reshape(1)
    place_far = lax.axis_index("zh").astype(jnp.int32).reshape(1)

    own_key = call(
        key_kernel,
        sds((EXP, BLOCKS, LANES), BF16),
        [VMEM, ANY],
        [pltpu.VMEM((BLOCKS, LANES), F32)],
    )(slot_keys, pltpu.with_memory_space_constraint(patches, pltpu.HBM))
    own_key, place_near, place_far = lax.optimization_barrier((own_key, place_near, place_far))
    keys = exchange(own_key, "x", "y", "core")
    terms, combine = call(
        dispatch_kernel,
        (tall_stats, sds((rows, EXP), BF16)),
        [SMEM, VMEM, VMEM],
        [pltpu.VMEM((EXP * BLOCKS, LANES), F32), pltpu.VMEM((EXP, D), BF16)],
    )(place_near, patches, keys)

    spread = [pltpu.VMEM((32 * SHARE, LANES), F32)]
    near = call(merge_near_kernel, wide_stats, [SMEM, VMEM])(place_far, exchange(terms, "zl", "core"))
    slot_tiles = call(merge_far_kernel, wide, [VMEM], spread)(exchange(near, "x", "zh"))
    out_terms = call(ffn_kernel, tall, [VMEM] * 3)(
        exchange(slot_tiles, "y", "zl"), jnp.swapaxes(w_in, 1, 2), w_out
    )
    near = call(add_near_kernel, wide, [VMEM])(exchange(out_terms, "zl", "core"))
    out_tiles = call(add_far_kernel, wide, [VMEM], spread)(exchange(near, "y", "zh"))
    return call(
        mix_kernel,
        sds((1, rows, D), BF16),
        [VMEM, VMEM],
        [pltpu.VMEM((rows, D), BF16), pltpu.SemaphoreType.DMA((SIDE,))],
        out_specs=ANY,
    )(exchange(out_tiles, "x", "zl"), combine)


def solution(mesh):
    split = Mesh(
        mesh.devices.reshape(SIDE, SIDE, SIDE, SIDE, CORES), ("zh", "zl", "x", "y", "core")
    )
    seq, exp = ("zh", "zl"), ("x", "y", "core")
    placed = (P(exp, seq, None), P(exp, None), P(exp, None, seq), P(exp, seq, None))
    return jax.shard_map(
        shards, mesh=split, in_specs=placed, out_specs=P(exp, seq, None), check_vma=False
    )
```

```python
import jax
import jax.numpy as jnp
from jax import lax
from jax.experimental import pallas as pl
from jax.experimental.pallas import tpu as pltpu
from jax.sharding import Mesh, PartitionSpec as P

F32 = jnp.float32
BF16 = jnp.bfloat16
SIDE = 4
CORES = 2
EXP = SIDE * SIDE * CORES
LANES = 128
D = 3072
BLOCKS = D // LANES
SHARE = BLOCKS // SIDE
PAIRS = SHARE // 2
PEERS = SIDE * SIDE
TALL = 16 * SHARE
WIDE = 8 * SHARE
VMEM = pl.BlockSpec(memory_space=pltpu.VMEM)
SMEM = pl.BlockSpec(memory_space=pltpu.SMEM)
ANY = pl.BlockSpec(memory_space=pl.ANY)
LIMIT = 24 * 1024 * 1024
sds = jax.ShapeDtypeStruct


def call(kernel, outs, in_specs, scratch=(), out_specs=None):
    return pl.pallas_call(
        kernel,
        out_shape=outs,
        in_specs=in_specs,
        out_specs=jax.tree.map(lambda _: VMEM, outs) if out_specs is None else out_specs,
        scratch_shapes=list(scratch),
        compiler_params=pltpu.CompilerParams(vmem_limit_bytes=LIMIT),
    )


def rows_top():
    return lax.broadcasted_iota(jnp.int32, (8, LANES), 0) < 4


def swap(x):
    return pltpu.roll(x, LANES // 2, 1)


def turn(x):
    return pltpu.roll(x, 4, 0)


def split_cores(tiles):
    top = rows_top()
    low = [jnp.where(top, tiles[a], turn(tiles[a + 1])) for a in (0, 2)]
    high = [jnp.where(top, turn(tiles[a]), tiles[a + 1]) for a in (0, 2)]
    return jnp.concatenate(low, axis=0), jnp.concatenate(high, axis=0)


def pick(g, low, high):
    a, b = (rows[8 * (g // 2) : 8 * (g // 2) + 8] for rows in (low, high))
    return jnp.where(rows_top(), a, turn(b)) if g % 2 == 0 else jnp.where(rows_top(), turn(a), b)


def store_share(out_ref, z, term):
    for c in range(CORES):
        for k in range(SHARE):
            piece = term[16 * c : 16 * c + 16, k * LANES : (k + 1) * LANES]
            out_ref[CORES * z + c, 16 * k : 16 * k + 16, :] = piece.astype(BF16)


def load_share(in_ref, z):
    columns = []
    for m in range(PAIRS):
        pairs = [in_ref[SIDE * g + z, 16 * m : 16 * m + 16, :].astype(F32) for g in range(SIDE)]
        columns.append(jnp.concatenate(split_cores([p[:8] for p in pairs]), axis=0))
        columns.append(jnp.concatenate(split_cores([p[8:] for p in pairs]), axis=0))
    return jnp.concatenate(columns, axis=1).astype(BF16)


def spread_stats(place, shift, denom):
    lane = lax.broadcasted_iota(jnp.int32, (shift.shape[0], LANES), 1)
    high = denom.astype(BF16).astype(F32)
    stats = jnp.where(lane == place, shift, 0.0)
    stats = jnp.where(lane == place + SIDE, high, stats)
    return jnp.where(lane == place + 2 * SIDE, denom - high, stats)


def merge_stats(stats):
    valid = lax.broadcasted_iota(jnp.int32, stats.shape, 1) < SIDE
    largest = jnp.max(jnp.where(valid, stats, -jnp.inf), axis=1, keepdims=True)
    scale = jnp.exp(jnp.where(valid, stats - largest, 0.0))
    parts = pltpu.roll(stats, LANES - SIDE, 1) + pltpu.roll(stats, LANES - 2 * SIDE, 1)
    denom = jnp.sum(jnp.where(valid, scale * parts, 0.0), axis=1, keepdims=True)
    return largest, scale, denom


def key_kernel(key_ref, patch_ref, out_ref, spread_ref):
    del patch_ref
    for k in range(BLOCKS):
        spread_ref[k : k + 1, :] = key_ref[:, k * LANES : (k + 1) * LANES].astype(F32)
    block = spread_ref[...].astype(BF16)
    for e in range(EXP):
        out_ref[e] = block


def dispatch_kernel(place_ref, patch_ref, keys_ref, out_ref, combine_ref, spread_ref, table_ref):
    spread_ref[...] = keys_ref[...].astype(F32).reshape(EXP * BLOCKS, LANES)
    for k in range(BLOCKS):
        for c in range(CORES):
            rows = spread_ref[pl.ds(BLOCKS * c + k, 16, stride=CORES * BLOCKS), :]
            table_ref[16 * c : 16 * c + 16, k * LANES : (k + 1) * LANES] = rows.astype(BF16)
    logits = lax.dot_general(
        table_ref[...], patch_ref[0], (((1,), (1,)), ((), ())), preferred_element_type=F32
    )
    shift = jnp.max(logits, axis=1, keepdims=True).astype(BF16).astype(F32)
    raised = jnp.exp(logits - shift)
    denom = jnp.sum(raised, axis=1, keepdims=True)
    weights = raised.astype(BF16)
    rest = (raised - weights.astype(F32)).astype(BF16)
    weights = jnp.concatenate([weights, rest], axis=0)
    stats = spread_stats(place_ref[0], shift, denom)
    for z in range(SIDE):
        base = z * SHARE * LANES
        columns = patch_ref[0, :, base : base + SHARE * LANES]
        term = jnp.dot(weights, columns, preferred_element_type=F32)
        store_share(out_ref, z, term[:EXP] + term[EXP:])
        for c in range(CORES):
            both = stats[16 * c : 16 * c + 8] + swap(stats[16 * c + 8 : 16 * c + 16])
            out_ref[CORES * z + c, TALL : TALL + 8, :] = both.astype(BF16)
    raised = jnp.exp(logits - jnp.max(logits, axis=0, keepdims=True))
    combine = raised / jnp.sum(raised, axis=0, keepdims=True)
    combine_ref[...] = combine.T.astype(BF16)


def sum_near(in_ref, out_ref, factor):
    for m in range(PAIRS):
        sums = []
        for k in (2 * m, 2 * m + 1):
            for c in range(CORES):
                total = None
                for z in range(SIDE):
                    rows = in_ref[CORES * z + c, 16 * k : 16 * k + 16, :].astype(F32)
                    if factor is not None:
                        rows = factor[c][z] * rows
                    total = rows if z == 0 else total + rows
                sums.append(total)
        for g in range(SIDE):
            pair = [pick(g, sums[0], sums[1]), pick(g, sums[2], sums[3])]
            pair = jnp.concatenate(pair, axis=0).astype(BF16)
            for h in range(SIDE):
                out_ref[SIDE * g + h, 16 * m : 16 * m + 16, :] = pair


def merge_near_kernel(place_ref, in_ref, out_ref):
    gathered = []
    for c in range(CORES):
        total = in_ref[c, TALL : TALL + 8, :].astype(F32)
        for z in range(1, SIDE):
            total += in_ref[CORES * z + c, TALL : TALL + 8, :].astype(F32)
        gathered += [total, swap(total)]
    largest, scale, denom = merge_stats(jnp.concatenate(gathered, axis=0))
    factor = [
        [jnp.broadcast_to(scale[16 * c : 16 * c + 16, z : z + 1], (16, LANES)) for z in range(SIDE)]
        for c in range(CORES)
    ]
    sum_near(in_ref, out_ref, factor)
    stats = spread_stats(place_ref[0], largest, denom)
    for g in range(SIDE):
        tile = pick(g, stats[:16], stats[16:]).astype(BF16)
        for h in range(SIDE):
            out_ref[SIDE * g + h, WIDE : WIDE + 8, :] = tile


def add_near_kernel(in_ref, out_ref):
    sum_near(in_ref, out_ref, None)


def sum_far(in_ref, out_ref, spread_ref, factor):
    for m in range(PAIRS):
        lows, highs = [], []
        for g in range(SIDE):
            low = high = None
            for h in range(SIDE):
                pair = in_ref[SIDE * g + h, 16 * m : 16 * m + 16, :].astype(F32)
                a, b = pair[:8], pair[8:]
                if factor is not None:
                    a, b = factor[g][h] * a, factor[g][h] * b
                low, high = (a, b) if h == 0 else (low + a, high + b)
            lows.append(low)
            highs.append(high)
        spread_ref[64 * m : 64 * m + 32, :] = jnp.concatenate(split_cores(lows), axis=0)
        spread_ref[64 * m + 32 : 64 * m + 64, :] = jnp.concatenate(split_cores(highs), axis=0)
    for g in range(SIDE):
        for m in range(PAIRS):
            low = spread_ref[pl.ds(64 * m + g, 8, stride=SIDE), :]
            high = spread_ref[pl.ds(64 * m + 32 + g, 8, stride=SIDE), :]
            pair = jnp.concatenate([low, high], axis=0).astype(BF16)
            for z in range(SIDE):
                out_ref[SIDE * g + z, 16 * m : 16 * m + 16, :] = pair


def merge_far_kernel(in_ref, out_ref, spread_ref):
    gathered = []
    for g in range(SIDE):
        total = in_ref[SIDE * g, WIDE : WIDE + 8, :].astype(F32)
        for h in range(1, SIDE):
            total += in_ref[SIDE * g + h, WIDE : WIDE + 8, :].astype(F32)
        gathered.append(total)
    _, scale, denom = merge_stats(jnp.concatenate(gathered, axis=0))
    scale = scale / denom
    factor = [
        [jnp.broadcast_to(scale[8 * g : 8 * g + 8, h : h + 1], (8, LANES)) for h in range(SIDE)]
        for g in range(SIDE)
    ]
    sum_far(in_ref, out_ref, spread_ref, factor)


def add_far_kernel(in_ref, out_ref, spread_ref):
    sum_far(in_ref, out_ref, spread_ref, None)


def ffn_kernel(in_ref, first_ref, second_ref, out_ref):
    hidden = None
    for z in range(SIDE):
        base = z * SHARE * LANES
        term = lax.dot_general(
            load_share(in_ref, z),
            first_ref[0, :, base : base + SHARE * LANES],
            (((1,), (1,)), ((), ())),
            preferred_element_type=F32,
        )
        hidden = term if z == 0 else hidden + term
    activated = jax.nn.gelu(hidden).astype(BF16)
    for z in range(SIDE):
        base = z * SHARE * LANES
        columns = second_ref[0, :, base : base + SHARE * LANES]
        store_share(out_ref, z, jnp.dot(activated, columns, preferred_element_type=F32))


def mix_kernel(in_ref, combine_ref, out_ref, mixed_ref, sems):
    copies = []
    for z in range(SIDE):
        columns = slice(z * SHARE * LANES, (z + 1) * SHARE * LANES)
        mixed_ref[:, columns] = jnp.dot(
            combine_ref[...], load_share(in_ref, z), preferred_element_type=F32
        ).astype(BF16)
        copy = pltpu.make_async_copy(mixed_ref.at[:, columns], out_ref.at[0, :, columns], sems.at[z])
        copy.start()
        copies.append(copy)
    for copy in copies:
        copy.wait()


def exchange(x, axes, groups=None):
    return lax.all_to_all(x, axes, split_axis=0, concat_axis=0, tiled=True, axis_index_groups=groups)


def column(h, z):
    return (z + 2 * (h // 2)) % SIDE


NEAR = [sorted((SIDE * h + z for z in range(SIDE)), key=lambda p: column(p // SIDE, p % SIDE)) for h in range(SIDE)]
FAR = [[near[z] for near in NEAR] for z in range(SIDE)]


def near_cores(x):
    groups = [[CORES * z + c for z in near for c in range(CORES)] for near in NEAR]
    return exchange(x, ("zh", "zl", "core"), groups)


def far(x, axis):
    groups = [[SIDE * z + g for g in range(SIDE) for z in far] for far in FAR]
    return exchange(x, ("zh", "zl", axis), groups)


def near(x, axis):
    groups = [[SIDE * z + g for g in range(SIDE) for z in near] for near in NEAR]
    return exchange(x, ("zh", "zl", axis), groups)


def shards(patches, slot_keys, w_in, w_out):
    rows = patches.shape[1]
    tall = sds((CORES * SIDE, TALL, LANES), BF16)
    tall_stats = sds((CORES * SIDE, TALL + 8, LANES), BF16)
    wide = sds((PEERS, WIDE, LANES), BF16)
    wide_stats = sds((PEERS, WIDE + 8, LANES), BF16)
    high, low = lax.axis_index("zh").astype(jnp.int32), lax.axis_index("zl").astype(jnp.int32)
    place_near, place_far = column(high, low).reshape(1), high.reshape(1)

    own_key = call(
        key_kernel,
        sds((EXP, BLOCKS, LANES), BF16),
        [VMEM, ANY],
        [pltpu.VMEM((BLOCKS, LANES), F32)],
    )(slot_keys, pltpu.with_memory_space_constraint(patches, pltpu.HBM))
    own_key, place_near, place_far = lax.optimization_barrier((own_key, place_near, place_far))
    keys = exchange(own_key, ("x", "y", "core"))
    terms, combine = call(
        dispatch_kernel,
        (tall_stats, sds((rows, EXP), BF16)),
        [SMEM, VMEM, VMEM],
        [pltpu.VMEM((EXP * BLOCKS, LANES), F32), pltpu.VMEM((EXP, D), BF16)],
    )(place_near, patches, keys)

    spread = [pltpu.VMEM((32 * SHARE, LANES), F32)]
    parts = call(merge_near_kernel, wide_stats, [SMEM, VMEM])(place_far, near_cores(terms))
    slot_tiles = call(merge_far_kernel, wide, [VMEM], spread)(far(parts, "x"))
    out_terms = call(ffn_kernel, tall, [VMEM] * 3)(
        near(slot_tiles, "y"), jnp.swapaxes(w_in, 1, 2), w_out
    )
    parts = call(add_near_kernel, wide, [VMEM])(near_cores(out_terms))
    out_tiles = call(add_far_kernel, wide, [VMEM], spread)(far(parts, "y"))
    return call(
        mix_kernel,
        sds((1, rows, D), BF16),
        [VMEM, VMEM],
        [pltpu.VMEM((rows, D), BF16), pltpu.SemaphoreType.DMA((SIDE,))],
        out_specs=ANY,
    )(near(out_tiles, "x"), combine)


def solution(mesh):
    split = Mesh(
        mesh.devices.reshape(SIDE, SIDE, SIDE, SIDE, CORES), ("zh", "zl", "x", "y", "core")
    )
    seq, exp = ("zh", "zl"), ("x", "y", "core")
    placed = (P(exp, seq, None), P(exp, None), P(exp, None, seq), P(exp, seq, None))
    return jax.shard_map(
        shards, mesh=split, in_specs=placed, out_specs=P(exp, seq, None), check_vma=False
    )
```

```python
import jax
import jax.numpy as jnp
from jax import lax
from jax.experimental import pallas as pl
from jax.experimental.pallas import tpu as pltpu
from jax.sharding import Mesh, PartitionSpec as P

F32 = jnp.float32
BF16 = jnp.bfloat16
SIDE = 4
CORES = 2
EXP = SIDE * SIDE * CORES
LANES = 128
D = 3072
BLOCKS = D // LANES
SHARE = BLOCKS // SIDE
PAIRS = SHARE // 2
PEERS = SIDE * SIDE
TALL = 16 * SHARE
WIDE = 8 * SHARE
VMEM = pl.BlockSpec(memory_space=pltpu.VMEM)
ANY = pl.BlockSpec(memory_space=pl.ANY)
LIMIT = 24 * 1024 * 1024
GROUP = 16
sds = jax.ShapeDtypeStruct


def call(kernel, outs, in_specs, scratch=(), out_specs=None):
    return pl.pallas_call(
        kernel,
        out_shape=outs,
        in_specs=in_specs,
        out_specs=jax.tree.map(lambda _: VMEM, outs) if out_specs is None else out_specs,
        scratch_shapes=list(scratch),
        compiler_params=pltpu.CompilerParams(vmem_limit_bytes=LIMIT),
    )


def rows_top():
    return lax.broadcasted_iota(jnp.int32, (8, LANES), 0) < 4


def swap(x):
    return pltpu.roll(x, LANES // 2, 1)


def turn(x):
    return pltpu.roll(x, 4, 0)


def split_cores(tiles):
    top = rows_top()
    low = [jnp.where(top, tiles[a], turn(tiles[a + 1])) for a in (0, 2)]
    high = [jnp.where(top, turn(tiles[a]), tiles[a + 1]) for a in (0, 2)]
    return jnp.concatenate(low, axis=0), jnp.concatenate(high, axis=0)


def pick(g, low, high):
    a, b = (rows[8 * (g // 2) : 8 * (g // 2) + 8] for rows in (low, high))
    return jnp.where(rows_top(), a, turn(b)) if g % 2 == 0 else jnp.where(rows_top(), turn(a), b)


def store_share(out_ref, z, term):
    for c in range(CORES):
        for k in range(SHARE):
            piece = term[16 * c : 16 * c + 16, k * LANES : (k + 1) * LANES]
            out_ref[CORES * z + c, 16 * k : 16 * k + 16, :] = piece.astype(BF16)


def load_share(in_ref, z):
    columns = []
    for m in range(PAIRS):
        pairs = [in_ref[SIDE * g + z, 16 * m : 16 * m + 16, :].astype(F32) for g in range(SIDE)]
        columns.append(jnp.concatenate(split_cores([p[:8] for p in pairs]), axis=0))
        columns.append(jnp.concatenate(split_cores([p[8:] for p in pairs]), axis=0))
    return jnp.concatenate(columns, axis=1).astype(BF16)


def lane_groups(rows):
    return lax.broadcasted_iota(jnp.int32, (rows, LANES), 1) % (LANES // 2) // GROUP


def join_stats(shift, high, rest):
    group = lane_groups(shift.shape[0])
    return jnp.where(group == 0, shift, jnp.where(group == 1, high, jnp.where(group == 2, rest, 0.0)))


def merge_stats(tiles):
    largest = jnp.maximum(jnp.maximum(tiles[0], tiles[1]), jnp.maximum(tiles[2], tiles[3]))
    scale = [jnp.exp(t - largest) for t in tiles]
    parts = [pltpu.roll(f, GROUP, 1) * (t + pltpu.roll(t, LANES - GROUP, 1)) for f, t in zip(scale, tiles)]
    return largest, scale, parts[0] + parts[1] + parts[2] + parts[3]


def all_lanes(x, lane):
    return jnp.broadcast_to(x[:, lane : lane + 1], x.shape)


def key_kernel(key_ref, patch_ref, out_ref, spread_ref):
    del patch_ref
    for k in range(BLOCKS):
        spread_ref[k : k + 1, :] = key_ref[:, k * LANES : (k + 1) * LANES].astype(F32)
    block = spread_ref[...].astype(BF16)
    for e in range(EXP):
        out_ref[e] = block


def dispatch_kernel(patch_ref, keys_ref, out_ref, combine_ref, spread_ref, table_ref):
    spread_ref[...] = keys_ref[...].astype(F32).reshape(EXP * BLOCKS, LANES)
    for k in range(BLOCKS):
        for c in range(CORES):
            rows = spread_ref[pl.ds(BLOCKS * c + k, 16, stride=CORES * BLOCKS), :]
            table_ref[16 * c : 16 * c + 16, k * LANES : (k + 1) * LANES] = rows.astype(BF16)
    half, deep = patch_ref.shape[1] // 2, D // 2
    logits = jnp.concatenate(
        [
            sum(
                lax.dot_general(
                    patch_ref[0, i * half : (i + 1) * half, k * deep : (k + 1) * deep],
                    table_ref[:, k * deep : (k + 1) * deep],
                    (((1,), (1,)), ((), ())),
                    preferred_element_type=F32,
                )
                for k in range(2)
            )
            for i in range(2)
        ],
        axis=0,
    ).T
    shift = jnp.max(logits, axis=1, keepdims=True).astype(BF16).astype(F32)
    raised = jnp.exp(logits - shift)
    denom = jnp.sum(raised, axis=1, keepdims=True)
    weights = raised.astype(BF16)
    rest = (raised - weights.astype(F32)).astype(BF16)
    weights = jnp.concatenate([weights, rest], axis=0)
    high = denom.astype(BF16).astype(F32)
    left = lax.broadcasted_iota(jnp.int32, (EXP, LANES), 1) < LANES // 2
    stats = jnp.where(left, join_stats(shift, high, denom - high), 0.0)
    for z in range(SIDE):
        base = z * SHARE * LANES
        columns = patch_ref[0, :, base : base + SHARE * LANES]
        term = jnp.dot(weights, columns, preferred_element_type=F32)
        store_share(out_ref, z, term[:EXP] + term[EXP:])
        for c in range(CORES):
            both = stats[16 * c : 16 * c + 8] + swap(stats[16 * c + 8 : 16 * c + 16])
            out_ref[CORES * z + c, TALL : TALL + 8, :] = both.astype(BF16)
    raised = jnp.exp(logits - jnp.max(logits, axis=0, keepdims=True))
    combine = raised / jnp.sum(raised, axis=0, keepdims=True)
    combine_ref[...] = combine.T.astype(BF16)


def sum_near(in_ref, out_ref, factor):
    for m in range(PAIRS):
        sums = []
        for k in (2 * m, 2 * m + 1):
            for c in range(CORES):
                total = None
                for z in range(SIDE):
                    rows = in_ref[CORES * z + c, 16 * k : 16 * k + 16, :].astype(F32)
                    if factor is not None:
                        rows = factor[c][z] * rows
                    total = rows if z == 0 else total + rows
                sums.append(total)
        for g in range(SIDE):
            pair = [pick(g, sums[0], sums[1]), pick(g, sums[2], sums[3])]
            pair = jnp.concatenate(pair, axis=0).astype(BF16)
            for h in range(SIDE):
                out_ref[SIDE * g + h, 16 * m : 16 * m + 16, :] = pair


def merge_near_kernel(in_ref, out_ref):
    factor, stats = [], []
    for c in range(CORES):
        tiles = [in_ref[CORES * z + c, TALL : TALL + 8, :].astype(F32) for z in range(SIDE)]
        largest, scale, denom = merge_stats(tiles)
        factor.append([jnp.concatenate([all_lanes(f, 0), all_lanes(f, LANES // 2)], axis=0) for f in scale])
        high = denom.astype(BF16).astype(F32)
        joined = join_stats(largest, high, pltpu.roll(denom - high, GROUP, 1))
        stats.append(jnp.concatenate([joined, swap(joined)], axis=0))
    sum_near(in_ref, out_ref, factor)
    for g in range(SIDE):
        tile = pick(g, stats[0], stats[1]).astype(BF16)
        for h in range(SIDE):
            out_ref[SIDE * g + h, WIDE : WIDE + 8, :] = tile


def add_near_kernel(in_ref, out_ref):
    sum_near(in_ref, out_ref, None)


def sum_far(in_ref, out_ref, spread_ref, factor):
    for m in range(PAIRS):
        lows, highs = [], []
        for g in range(SIDE):
            low = high = None
            for h in range(SIDE):
                pair = in_ref[SIDE * g + h, 16 * m : 16 * m + 16, :].astype(F32)
                a, b = pair[:8], pair[8:]
                if factor is not None:
                    a, b = factor[g][h] * a, factor[g][h] * b
                low, high = (a, b) if h == 0 else (low + a, high + b)
            lows.append(low)
            highs.append(high)
        spread_ref[64 * m : 64 * m + 32, :] = jnp.concatenate(split_cores(lows), axis=0)
        spread_ref[64 * m + 32 : 64 * m + 64, :] = jnp.concatenate(split_cores(highs), axis=0)
    for g in range(SIDE):
        for m in range(PAIRS):
            low = spread_ref[pl.ds(64 * m + g, 8, stride=SIDE), :]
            high = spread_ref[pl.ds(64 * m + 32 + g, 8, stride=SIDE), :]
            pair = jnp.concatenate([low, high], axis=0).astype(BF16)
            for z in range(SIDE):
                out_ref[SIDE * g + z, 16 * m : 16 * m + 16, :] = pair


def merge_far_kernel(in_ref, out_ref, spread_ref):
    factor = []
    for g in range(SIDE):
        tiles = [in_ref[SIDE * g + h, WIDE : WIDE + 8, :].astype(F32) for h in range(SIDE)]
        _, scale, denom = merge_stats(tiles)
        inverse = pltpu.roll(1.0 / denom, LANES - GROUP, 1)
        factor.append([all_lanes(f * inverse, 0) for f in scale])
    sum_far(in_ref, out_ref, spread_ref, factor)


def add_far_kernel(in_ref, out_ref, spread_ref):
    sum_far(in_ref, out_ref, spread_ref, None)


def ffn_kernel(in_ref, first_ref, second_ref, out_ref):
    hidden = None
    part = first_ref.shape[1] // 4
    for k in range(2):
        rows = jnp.concatenate([load_share(in_ref, 2 * k), load_share(in_ref, 2 * k + 1)], axis=1)
        terms = [
            lax.dot_general(
                rows,
                first_ref[0, i * part : (i + 1) * part, k * D // 2 : (k + 1) * D // 2],
                (((1,), (1,)), ((), ())),
                preferred_element_type=F32,
            )
            for i in range(4)
        ]
        term = jnp.concatenate(terms, axis=1)
        hidden = term if k == 0 else hidden + term
    activated = jax.nn.gelu(hidden).astype(BF16)
    for z in range(SIDE):
        base = z * SHARE * LANES
        columns = second_ref[0, :, base : base + SHARE * LANES]
        store_share(out_ref, z, jnp.dot(activated, columns, preferred_element_type=F32))


def mix_kernel(in_ref, combine_ref, out_ref, mixed_ref, sems):
    copies = []
    for z in range(SIDE):
        columns = slice(z * SHARE * LANES, (z + 1) * SHARE * LANES)
        mixed_ref[:, columns] = jnp.dot(
            combine_ref[...], load_share(in_ref, z), preferred_element_type=F32
        ).astype(BF16)
        copy = pltpu.make_async_copy(mixed_ref.at[:, columns], out_ref.at[0, :, columns], sems.at[z])
        copy.start()
        copies.append(copy)
    for copy in copies:
        copy.wait()


def exchange(x, axes, groups=None):
    return lax.all_to_all(x, axes, split_axis=0, concat_axis=0, tiled=True, axis_index_groups=groups)


def column(h, z):
    return (z + 2 * (h // 2)) % SIDE


NEAR = [sorted((SIDE * h + z for z in range(SIDE)), key=lambda p: column(p // SIDE, p % SIDE)) for h in range(SIDE)]
FAR = [[near[z] for near in NEAR] for z in range(SIDE)]


def near_cores(x):
    groups = [[CORES * z + c for z in near for c in range(CORES)] for near in NEAR]
    return exchange(x, ("zh", "zl", "core"), groups)


def far(x, axis):
    groups = [[SIDE * z + g for g in range(SIDE) for z in far] for far in FAR]
    return exchange(x, ("zh", "zl", axis), groups)


def near(x, axis):
    groups = [[SIDE * z + g for g in range(SIDE) for z in near] for near in NEAR]
    return exchange(x, ("zh", "zl", axis), groups)


def shards(patches, slot_keys, w_in, w_out):
    rows = patches.shape[1]
    tall = sds((CORES * SIDE, TALL, LANES), BF16)
    tall_stats = sds((CORES * SIDE, TALL + 8, LANES), BF16)
    wide = sds((PEERS, WIDE, LANES), BF16)
    wide_stats = sds((PEERS, WIDE + 8, LANES), BF16)

    own_key = call(
        key_kernel,
        sds((EXP, BLOCKS, LANES), BF16),
        [VMEM, ANY],
        [pltpu.VMEM((BLOCKS, LANES), F32)],
    )(slot_keys, pltpu.with_memory_space_constraint(patches, pltpu.HBM))
    keys = exchange(own_key, ("x", "y", "core"))
    terms, combine = call(
        dispatch_kernel,
        (tall_stats, sds((rows, EXP), BF16)),
        [VMEM, VMEM],
        [pltpu.VMEM((EXP * BLOCKS, LANES), F32), pltpu.VMEM((EXP, D), BF16)],
    )(patches, keys)

    spread = [pltpu.VMEM((32 * SHARE, LANES), F32)]
    parts = call(merge_near_kernel, wide_stats, [VMEM])(near_cores(terms))
    slot_tiles = call(merge_far_kernel, wide, [VMEM], spread)(far(parts, "x"))
    out_terms = call(ffn_kernel, tall, [VMEM] * 3)(
        near(slot_tiles, "y"), jnp.swapaxes(w_in, 1, 2), w_out
    )
    parts = call(add_near_kernel, wide, [VMEM])(near_cores(out_terms))
    out_tiles = call(add_far_kernel, wide, [VMEM], spread)(far(parts, "y"))
    return call(
        mix_kernel,
        sds((1, rows, D), BF16),
        [VMEM, VMEM],
        [pltpu.VMEM((rows, D), BF16), pltpu.SemaphoreType.DMA((SIDE,))],
        out_specs=ANY,
    )(near(out_tiles, "x"), combine)


def solution(mesh):
    split = Mesh(
        mesh.devices.reshape(SIDE, SIDE, SIDE, SIDE, CORES), ("zh", "zl", "x", "y", "core")
    )
    seq, exp = ("zh", "zl"), ("x", "y", "core")
    placed = (P(exp, seq, None), P(exp, None), P(exp, None, seq), P(exp, seq, None))
    return jax.shard_map(
        shards, mesh=split, in_specs=placed, out_specs=P(exp, seq, None), check_vma=False
    )
```

```python
import jax
import jax.numpy as jnp
from jax import lax
from jax.experimental import pallas as pl
from jax.experimental.pallas import tpu as pltpu
from jax.sharding import Mesh, PartitionSpec as P

F32 = jnp.float32
BF16 = jnp.bfloat16
SIDE = 4
CORES = 2
EXP = SIDE * SIDE * CORES
LANES = 128
D = 3072
BLOCKS = D // LANES
SHARE = BLOCKS // SIDE
PAIRS = SHARE // 2
PEERS = SIDE * SIDE
TALL = 16 * SHARE
WIDE = 8 * SHARE
FLAT = (CORES * SHARE + 1) * LANES
VMEM = pl.BlockSpec(memory_space=pltpu.VMEM)
ANY = pl.BlockSpec(memory_space=pl.ANY)
LIMIT = 24 * 1024 * 1024
GROUP = 16
sds = jax.ShapeDtypeStruct


def call(kernel, outs, in_specs, scratch=(), out_specs=None):
    return pl.pallas_call(
        kernel,
        out_shape=outs,
        in_specs=in_specs,
        out_specs=jax.tree.map(lambda _: VMEM, outs) if out_specs is None else out_specs,
        scratch_shapes=list(scratch),
        compiler_params=pltpu.CompilerParams(vmem_limit_bytes=LIMIT),
    )


def rows_top():
    return lax.broadcasted_iota(jnp.int32, (8, LANES), 0) < 4


def swap(x):
    return pltpu.roll(x, LANES // 2, 1)


def turn(x):
    return pltpu.roll(x, 4, 0)


def split_cores(tiles):
    top = rows_top()
    low = [jnp.where(top, tiles[a], turn(tiles[a + 1])) for a in (0, 2)]
    high = [jnp.where(top, turn(tiles[a]), tiles[a + 1]) for a in (0, 2)]
    return jnp.concatenate(low, axis=0), jnp.concatenate(high, axis=0)


def pick(g, low, high):
    a, b = (rows[8 * (g // 2) : 8 * (g // 2) + 8] for rows in (low, high))
    return jnp.where(rows_top(), a, turn(b)) if g % 2 == 0 else jnp.where(rows_top(), turn(a), b)


def store_share(out_ref, z, term):
    for c in range(CORES):
        for k in range(SHARE):
            piece = term[16 * c : 16 * c + 16, k * LANES : (k + 1) * LANES]
            out_ref[CORES * z + c, 16 * k : 16 * k + 16, :] = piece.astype(BF16)


def load_share(in_ref, z):
    columns = []
    for m in range(PAIRS):
        pairs = [in_ref[SIDE * g + z, 16 * m : 16 * m + 16, :].astype(F32) for g in range(SIDE)]
        columns.append(jnp.concatenate(split_cores([p[:8] for p in pairs]), axis=0))
        columns.append(jnp.concatenate(split_cores([p[8:] for p in pairs]), axis=0))
    return jnp.concatenate(columns, axis=1).astype(BF16)


def lane_groups(rows):
    return lax.broadcasted_iota(jnp.int32, (rows, LANES), 1) % (LANES // 2) // GROUP


def join_stats(shift, high, rest):
    group = lane_groups(shift.shape[0])
    return jnp.where(group == 0, shift, jnp.where(group == 1, high, jnp.where(group == 2, rest, 0.0)))


def merge_stats(tiles):
    largest = jnp.maximum(jnp.maximum(tiles[0], tiles[1]), jnp.maximum(tiles[2], tiles[3]))
    scale = [jnp.exp(t - largest) for t in tiles]
    parts = [pltpu.roll(f, GROUP, 1) * (t + pltpu.roll(t, LANES - GROUP, 1)) for f, t in zip(scale, tiles)]
    return largest, scale, parts[0] + parts[1] + parts[2] + parts[3]


def all_lanes(x, lane):
    return jnp.broadcast_to(x[:, lane : lane + 1], x.shape)


def key_kernel(key_ref, patch_ref, out_ref, spread_ref):
    del patch_ref
    for k in range(BLOCKS):
        spread_ref[k : k + 1, :] = key_ref[:, k * LANES : (k + 1) * LANES].astype(F32)
    block = spread_ref[...].astype(BF16)
    for e in range(EXP):
        out_ref[e] = block


def dispatch_kernel(patch_ref, keys_ref, out_ref, combine_ref, spread_ref, table_ref):
    spread_ref[...] = keys_ref[...].astype(F32).reshape(EXP * BLOCKS, LANES)
    for k in range(BLOCKS):
        for c in range(CORES):
            rows = spread_ref[pl.ds(BLOCKS * c + k, 16, stride=CORES * BLOCKS), :]
            table_ref[16 * c : 16 * c + 16, k * LANES : (k + 1) * LANES] = rows.astype(BF16)
    half, deep = patch_ref.shape[1] // 2, D // 2
    logits = jnp.concatenate(
        [
            sum(
                lax.dot_general(
                    patch_ref[0, i * half : (i + 1) * half, k * deep : (k + 1) * deep],
                    table_ref[:, k * deep : (k + 1) * deep],
                    (((1,), (1,)), ((), ())),
                    preferred_element_type=F32,
                )
                for k in range(2)
            )
            for i in range(2)
        ],
        axis=0,
    ).T
    shift = jnp.max(logits, axis=1, keepdims=True).astype(BF16).astype(F32)
    raised = jnp.exp(logits - shift)
    denom = jnp.sum(raised, axis=1, keepdims=True)
    weights = raised.astype(BF16)
    rest = (raised - weights.astype(F32)).astype(BF16)
    weights = jnp.concatenate([weights, rest], axis=0)
    high = denom.astype(BF16).astype(F32)
    left = lax.broadcasted_iota(jnp.int32, (EXP, LANES), 1) < LANES // 2
    stats = jnp.where(left, join_stats(shift, high, denom - high), 0.0)
    for z in range(SIDE):
        base = z * SHARE * LANES
        columns = patch_ref[0, :, base : base + SHARE * LANES]
        term = jnp.dot(weights, columns, preferred_element_type=F32)
        store_share(out_ref, z, term[:EXP] + term[EXP:])
        for c in range(CORES):
            both = stats[16 * c : 16 * c + 8] + swap(stats[16 * c + 8 : 16 * c + 16])
            out_ref[CORES * z + c, TALL : TALL + 8, :] = both.astype(BF16)
    raised = jnp.exp(logits - jnp.max(logits, axis=0, keepdims=True))
    combine = raised / jnp.sum(raised, axis=0, keepdims=True)
    combine_ref[...] = combine.T.astype(BF16)


def near_total(in_ref, c, k, factor):
    total = None
    for z in range(SIDE):
        rows = in_ref[CORES * z + c, 16 * k : 16 * k + 16, :].astype(F32)
        if factor is not None:
            rows = factor[c][z] * rows
        total = rows if z == 0 else total + rows
    return total


def merge_near_kernel(in_ref, out_ref):
    factor, stats = [], []
    for c in range(CORES):
        tiles = [in_ref[CORES * z + c, TALL : TALL + 8, :].astype(F32) for z in range(SIDE)]
        largest, scale, denom = merge_stats(tiles)
        factor.append([jnp.concatenate([all_lanes(f, 0), all_lanes(f, LANES // 2)], axis=0) for f in scale])
        high = denom.astype(BF16).astype(F32)
        joined = join_stats(largest, high, pltpu.roll(denom - high, GROUP, 1))
        stats.append(jnp.concatenate([joined, swap(joined)], axis=0))
    for k in range(SHARE):
        for c in range(CORES):
            total = near_total(in_ref, c, k, factor).astype(BF16)
            lanes = slice((CORES * k + c) * LANES, (CORES * k + c + 1) * LANES)
            for g in range(SIDE):
                for h in range(SIDE):
                    out_ref[SIDE * g + h, :, lanes] = total[4 * g : 4 * g + 4]
    left = lax.broadcasted_iota(jnp.int32, (16, LANES), 1) < LANES // 2
    both = jnp.where(left, stats[0], swap(stats[1])).astype(BF16)
    for g in range(SIDE):
        for h in range(SIDE):
            out_ref[SIDE * g + h, :, FLAT - LANES :] = both[4 * g : 4 * g + 4]


def add_near_kernel(in_ref, out_ref):
    for m in range(PAIRS):
        sums = [near_total(in_ref, c, k, None) for k in (2 * m, 2 * m + 1) for c in range(CORES)]
        for g in range(SIDE):
            pair = [pick(g, sums[0], sums[1]), pick(g, sums[2], sums[3])]
            pair = jnp.concatenate(pair, axis=0).astype(BF16)
            for h in range(SIDE):
                out_ref[SIDE * g + h, 16 * m : 16 * m + 16, :] = pair


def store_turned(out_ref, spread_ref):
    for g in range(SIDE):
        for m in range(PAIRS):
            low = spread_ref[pl.ds(64 * m + g, 8, stride=SIDE), :]
            high = spread_ref[pl.ds(64 * m + 32 + g, 8, stride=SIDE), :]
            pair = jnp.concatenate([low, high], axis=0).astype(BF16)
            for z in range(SIDE):
                out_ref[SIDE * g + z, 16 * m : 16 * m + 16, :] = pair


def merge_far_kernel(in_ref, out_ref, spread_ref):
    factor = []
    for g in range(SIDE):
        tiles = [in_ref[SIDE * g + h, :, FLAT - LANES :].astype(F32) for h in range(SIDE)]
        _, scale, denom = merge_stats(tiles)
        inverse = pltpu.roll(1.0 / denom, LANES - GROUP, 1)
        scale = [f * inverse for f in scale]
        factor.append([[all_lanes(f, c * (LANES // 2)) for f in scale] for c in range(CORES)])
    for k in range(SHARE):
        for c in range(CORES):
            lanes = slice((CORES * k + c) * LANES, (CORES * k + c + 1) * LANES)
            for g in range(SIDE):
                total = None
                for h in range(SIDE):
                    rows = factor[g][c][h] * in_ref[SIDE * g + h, :, lanes].astype(F32)
                    total = rows if h == 0 else total + rows
                first = 32 * k + 16 * c + 4 * g
                spread_ref[first : first + 4, :] = total
    store_turned(out_ref, spread_ref)


def add_far_kernel(in_ref, out_ref, spread_ref):
    for m in range(PAIRS):
        lows, highs = [], []
        for g in range(SIDE):
            pairs = [in_ref[SIDE * g + h, 16 * m : 16 * m + 16, :].astype(F32) for h in range(SIDE)]
            total = pairs[0] + pairs[1] + pairs[2] + pairs[3]
            lows.append(total[:8])
            highs.append(total[8:])
        spread_ref[64 * m : 64 * m + 32, :] = jnp.concatenate(split_cores(lows), axis=0)
        spread_ref[64 * m + 32 : 64 * m + 64, :] = jnp.concatenate(split_cores(highs), axis=0)
    store_turned(out_ref, spread_ref)


def ffn_kernel(in_ref, first_ref, second_ref, out_ref):
    hidden = None
    part = first_ref.shape[1] // 4
    for k in range(2):
        rows = jnp.concatenate([load_share(in_ref, 2 * k), load_share(in_ref, 2 * k + 1)], axis=1)
        terms = [
            lax.dot_general(
                rows,
                first_ref[0, i * part : (i + 1) * part, k * D // 2 : (k + 1) * D // 2],
                (((1,), (1,)), ((), ())),
                preferred_element_type=F32,
            )
            for i in range(4)
        ]
        term = jnp.concatenate(terms, axis=1)
        hidden = term if k == 0 else hidden + term
    activated = jax.nn.gelu(hidden).astype(BF16)
    for z in range(SIDE):
        base = z * SHARE * LANES
        columns = second_ref[0, :, base : base + SHARE * LANES]
        store_share(out_ref, z, jnp.dot(activated, columns, preferred_element_type=F32))


def mix_kernel(in_ref, combine_ref, out_ref, mixed_ref, sems):
    copies = []
    for z in range(SIDE):
        columns = slice(z * SHARE * LANES, (z + 1) * SHARE * LANES)
        mixed_ref[:, columns] = jnp.dot(
            combine_ref[...], load_share(in_ref, z), preferred_element_type=F32
        ).astype(BF16)
        copy = pltpu.make_async_copy(mixed_ref.at[:, columns], out_ref.at[0, :, columns], sems.at[z])
        copy.start()
        copies.append(copy)
    for copy in copies:
        copy.wait()


def exchange(x, axes, groups=None):
    return lax.all_to_all(x, axes, split_axis=0, concat_axis=0, tiled=True, axis_index_groups=groups)


def column(h, z):
    return (z + 2 * (h // 2)) % SIDE


NEAR = [sorted((SIDE * h + z for z in range(SIDE)), key=lambda p: column(p // SIDE, p % SIDE)) for h in range(SIDE)]
FAR = [[near[z] for near in NEAR] for z in range(SIDE)]


def near_cores(x):
    groups = [[CORES * z + c for z in near for c in range(CORES)] for near in NEAR]
    return exchange(x, ("zh", "zl", "core"), groups)


def far(x, axis):
    groups = [[SIDE * z + g for g in range(SIDE) for z in far] for far in FAR]
    return exchange(x, ("zh", "zl", axis), groups)


def near(x, axis):
    groups = [[SIDE * z + g for g in range(SIDE) for z in near] for near in NEAR]
    return exchange(x, ("zh", "zl", axis), groups)


def shards(patches, slot_keys, w_in, w_out):
    rows = patches.shape[1]
    tall = sds((CORES * SIDE, TALL, LANES), BF16)
    tall_stats = sds((CORES * SIDE, TALL + 8, LANES), BF16)
    wide = sds((PEERS, WIDE, LANES), BF16)
    flat_stats = sds((PEERS, 4, FLAT), BF16)

    own_key = call(
        key_kernel,
        sds((EXP, BLOCKS, LANES), BF16),
        [VMEM, ANY],
        [pltpu.VMEM((BLOCKS, LANES), F32)],
    )(slot_keys, pltpu.with_memory_space_constraint(patches, pltpu.HBM))
    keys = exchange(own_key, ("x", "y", "core"))
    terms, combine = call(
        dispatch_kernel,
        (tall_stats, sds((rows, EXP), BF16)),
        [VMEM, VMEM],
        [pltpu.VMEM((EXP * BLOCKS, LANES), F32), pltpu.VMEM((EXP, D), BF16)],
    )(patches, keys)

    spread = [pltpu.VMEM((32 * SHARE, LANES), F32)]
    parts = call(merge_near_kernel, flat_stats, [VMEM])(near_cores(terms))
    slot_tiles = call(merge_far_kernel, wide, [VMEM], spread)(far(parts, "x"))
    out_terms = call(ffn_kernel, tall, [VMEM] * 3)(
        near(slot_tiles, "y"), jnp.swapaxes(w_in, 1, 2), w_out
    )
    parts = call(add_near_kernel, wide, [VMEM])(near_cores(out_terms))
    out_tiles = call(add_far_kernel, wide, [VMEM], spread)(far(parts, "y"))
    return call(
        mix_kernel,
        sds((1, rows, D), BF16),
        [VMEM, VMEM],
        [pltpu.VMEM((rows, D), BF16), pltpu.SemaphoreType.DMA((SIDE,))],
        out_specs=ANY,
    )(near(out_tiles, "x"), combine)


def solution(mesh):
    split = Mesh(
        mesh.devices.reshape(SIDE, SIDE, SIDE, SIDE, CORES), ("zh", "zl", "x", "y", "core")
    )
    seq, exp = ("zh", "zl"), ("x", "y", "core")
    placed = (P(exp, seq, None), P(exp, None), P(exp, None, seq), P(exp, seq, None))
    return jax.shard_map(
        shards, mesh=split, in_specs=placed, out_specs=P(exp, seq, None), check_vma=False
    )
```

```python
import jax
import jax.numpy as jnp
from jax import lax
from jax.experimental import pallas as pl
from jax.experimental.pallas import tpu as pltpu
from jax.sharding import Mesh, PartitionSpec as P

F32 = jnp.float32
BF16 = jnp.bfloat16
SIDE = 4
CORES = 2
EXP = SIDE * SIDE * CORES
LANES = 128
D = 3072
BLOCKS = D // LANES
SHARE = BLOCKS // SIDE
PAIRS = SHARE // 2
PEERS = SIDE * SIDE
TALL = 16 * SHARE
WIDE = 8 * SHARE
FLAT = (CORES * SHARE + 1) * LANES
VMEM = pl.BlockSpec(memory_space=pltpu.VMEM)
ANY = pl.BlockSpec(memory_space=pl.ANY)
LIMIT = 24 * 1024 * 1024
GROUP = 16
sds = jax.ShapeDtypeStruct


def call(kernel, outs, in_specs, scratch=(), out_specs=None):
    return pl.pallas_call(
        kernel,
        out_shape=outs,
        in_specs=in_specs,
        out_specs=jax.tree.map(lambda _: VMEM, outs) if out_specs is None else out_specs,
        scratch_shapes=list(scratch),
        compiler_params=pltpu.CompilerParams(vmem_limit_bytes=LIMIT),
    )


def rows_top():
    return lax.broadcasted_iota(jnp.int32, (8, LANES), 0) < 4


def swap(x):
    return pltpu.roll(x, LANES // 2, 1)


def turn(x):
    return pltpu.roll(x, 4, 0)


def split_cores(tiles):
    top = rows_top()
    low = [jnp.where(top, tiles[a], turn(tiles[a + 1])) for a in (0, 2)]
    high = [jnp.where(top, turn(tiles[a]), tiles[a + 1]) for a in (0, 2)]
    return jnp.concatenate(low, axis=0), jnp.concatenate(high, axis=0)


def pick(g, low, high):
    a, b = (rows[8 * (g // 2) : 8 * (g // 2) + 8] for rows in (low, high))
    return jnp.where(rows_top(), a, turn(b)) if g % 2 == 0 else jnp.where(rows_top(), turn(a), b)


def store_share(out_ref, z, term):
    for c in range(CORES):
        for k in range(SHARE):
            piece = term[16 * c : 16 * c + 16, k * LANES : (k + 1) * LANES]
            out_ref[CORES * z + c, 16 * k : 16 * k + 16, :] = piece.astype(BF16)


def load_share(in_ref, z):
    columns = []
    for m in range(PAIRS):
        pairs = [in_ref[SIDE * g + z, 16 * m : 16 * m + 16, :].astype(F32) for g in range(SIDE)]
        columns.append(jnp.concatenate(split_cores([p[:8] for p in pairs]), axis=0))
        columns.append(jnp.concatenate(split_cores([p[8:] for p in pairs]), axis=0))
    return jnp.concatenate(columns, axis=1).astype(BF16)


def lane_groups(rows):
    return lax.broadcasted_iota(jnp.int32, (rows, LANES), 1) % (LANES // 2) // GROUP


def join_stats(shift, high, rest):
    group = lane_groups(shift.shape[0])
    return jnp.where(group == 0, shift, jnp.where(group == 1, high, jnp.where(group == 2, rest, 0.0)))


def merge_stats(tiles):
    largest = jnp.maximum(jnp.maximum(tiles[0], tiles[1]), jnp.maximum(tiles[2], tiles[3]))
    scale = [jnp.exp(t - largest) for t in tiles]
    parts = [pltpu.roll(f, GROUP, 1) * (t + pltpu.roll(t, LANES - GROUP, 1)) for f, t in zip(scale, tiles)]
    return largest, scale, parts[0] + parts[1] + parts[2] + parts[3]


def all_lanes(x, lane):
    return jnp.broadcast_to(x[:, lane : lane + 1], x.shape)


def key_kernel(key_ref, patch_ref, out_ref, spread_ref):
    del patch_ref
    for k in range(BLOCKS):
        spread_ref[k : k + 1, :] = key_ref[:, k * LANES : (k + 1) * LANES].astype(F32)
    block = spread_ref[...].astype(BF16)
    for e in range(EXP):
        out_ref[e] = block


def dispatch_kernel(patch_ref, keys_ref, out_ref, combine_ref, spread_ref, table_ref):
    spread_ref[...] = keys_ref[...].astype(F32).reshape(EXP * BLOCKS, LANES)
    for k in range(BLOCKS):
        for c in range(CORES):
            rows = spread_ref[pl.ds(BLOCKS * c + k, 16, stride=CORES * BLOCKS), :]
            table_ref[16 * c : 16 * c + 16, k * LANES : (k + 1) * LANES] = rows.astype(BF16)
    half, deep = patch_ref.shape[1] // 2, D // 2
    logits = jnp.concatenate(
        [
            sum(
                lax.dot_general(
                    patch_ref[0, i * half : (i + 1) * half, k * deep : (k + 1) * deep],
                    table_ref[:, k * deep : (k + 1) * deep],
                    (((1,), (1,)), ((), ())),
                    preferred_element_type=F32,
                )
                for k in range(2)
            )
            for i in range(2)
        ],
        axis=0,
    ).T
    shift = jnp.max(logits, axis=1, keepdims=True).astype(BF16).astype(F32)
    raised = jnp.exp(logits - shift)
    denom = jnp.sum(raised, axis=1, keepdims=True)
    weights = raised.astype(BF16)
    rest = (raised - weights.astype(F32)).astype(BF16)
    weights = jnp.concatenate([weights, rest], axis=0)
    high = denom.astype(BF16).astype(F32)
    left = lax.broadcasted_iota(jnp.int32, (EXP, LANES), 1) < LANES // 2
    stats = jnp.where(left, join_stats(shift, high, denom - high), 0.0)
    for z in range(SIDE):
        base = z * SHARE * LANES
        columns = patch_ref[0, :, base : base + SHARE * LANES]
        term = jnp.dot(weights, columns, preferred_element_type=F32)
        store_share(out_ref, z, term[:EXP] + term[EXP:])
        for c in range(CORES):
            both = stats[16 * c : 16 * c + 8] + swap(stats[16 * c + 8 : 16 * c + 16])
            out_ref[CORES * z + c, TALL : TALL + 8, :] = both.astype(BF16)
    raised = jnp.exp(logits - jnp.max(logits, axis=0, keepdims=True))
    combine = raised / jnp.sum(raised, axis=0, keepdims=True)
    combine_ref[...] = combine.T.astype(BF16)


def near_total(in_ref, c, k, factor):
    total = None
    for z in range(SIDE):
        rows = in_ref[CORES * z + c, 16 * k : 16 * k + 16, :].astype(F32)
        if factor is not None:
            rows = factor[c][z] * rows
        total = rows if z == 0 else total + rows
    return total


def merge_near_kernel(in_ref, out_ref):
    factor, stats = [], []
    for c in range(CORES):
        tiles = [in_ref[CORES * z + c, TALL : TALL + 8, :].astype(F32) for z in range(SIDE)]
        largest, scale, denom = merge_stats(tiles)
        factor.append([jnp.concatenate([all_lanes(f, 0), all_lanes(f, LANES // 2)], axis=0) for f in scale])
        high = denom.astype(BF16).astype(F32)
        joined = join_stats(largest, high, pltpu.roll(denom - high, GROUP, 1))
        stats.append(jnp.concatenate([joined, swap(joined)], axis=0))
    for k in range(SHARE):
        for c in range(CORES):
            total = near_total(in_ref, c, k, factor).astype(BF16)
            lanes = slice((CORES * k + c) * LANES, (CORES * k + c + 1) * LANES)
            for g in range(SIDE):
                for h in range(SIDE):
                    out_ref[SIDE * g + h, :, lanes] = total[4 * g : 4 * g + 4]
    left = lax.broadcasted_iota(jnp.int32, (16, LANES), 1) < LANES // 2
    both = jnp.where(left, stats[0], swap(stats[1])).astype(BF16)
    for g in range(SIDE):
        for h in range(SIDE):
            out_ref[SIDE * g + h, :, FLAT - LANES :] = both[4 * g : 4 * g + 4]


def add_near_kernel(in_ref, out_ref):
    for m in range(PAIRS):
        sums = [near_total(in_ref, c, k, None) for k in (2 * m, 2 * m + 1) for c in range(CORES)]
        for g in range(SIDE):
            pair = [pick(g, sums[0], sums[1]), pick(g, sums[2], sums[3])]
            pair = jnp.concatenate(pair, axis=0).astype(BF16)
            for h in range(SIDE):
                out_ref[SIDE * g + h, 16 * m : 16 * m + 16, :] = pair


def store_turned(out_ref, spread_ref):
    for g in range(SIDE):
        for m in range(PAIRS):
            low = spread_ref[pl.ds(64 * m + g, 8, stride=SIDE), :]
            high = spread_ref[pl.ds(64 * m + 32 + g, 8, stride=SIDE), :]
            pair = jnp.concatenate([low, high], axis=0).astype(BF16)
            for z in range(SIDE):
                out_ref[SIDE * g + z, 16 * m : 16 * m + 16, :] = pair


def merge_far_kernel(in_ref, out_ref, spread_ref):
    factor = []
    for g in range(SIDE):
        tiles = [in_ref[SIDE * g + h, :, FLAT - LANES :].astype(F32) for h in range(SIDE)]
        _, scale, denom = merge_stats(tiles)
        inverse = pltpu.roll(1.0 / denom, LANES - GROUP, 1)
        scale = [f * inverse for f in scale]
        factor.append([[all_lanes(f, c * (LANES // 2)) for f in scale] for c in range(CORES)])
    for k in range(SHARE):
        for c in range(CORES):
            lanes = slice((CORES * k + c) * LANES, (CORES * k + c + 1) * LANES)
            for g in range(SIDE):
                total = None
                for h in range(SIDE):
                    rows = factor[g][c][h] * in_ref[SIDE * g + h, :, lanes].astype(F32)
                    total = rows if h == 0 else total + rows
                first = 32 * k + 16 * c + 4 * g
                spread_ref[first : first + 4, :] = total
    store_turned(out_ref, spread_ref)


def add_far_kernel(in_ref, out_ref, spread_ref):
    for m in range(PAIRS):
        lows, highs = [], []
        for g in range(SIDE):
            pairs = [in_ref[SIDE * g + h, 16 * m : 16 * m + 16, :].astype(F32) for h in range(SIDE)]
            total = pairs[0] + pairs[1] + pairs[2] + pairs[3]
            lows.append(total[:8])
            highs.append(total[8:])
        spread_ref[64 * m : 64 * m + 32, :] = jnp.concatenate(split_cores(lows), axis=0)
        spread_ref[64 * m + 32 : 64 * m + 64, :] = jnp.concatenate(split_cores(highs), axis=0)
    store_turned(out_ref, spread_ref)


def ffn_kernel(in_ref, first_ref, second_ref, out_ref):
    hidden = None
    part = first_ref.shape[1] // 4
    for k in range(2):
        rows = jnp.concatenate([load_share(in_ref, 2 * k), load_share(in_ref, 2 * k + 1)], axis=1)
        terms = [
            lax.dot_general(
                rows,
                first_ref[0, i * part : (i + 1) * part, k * D // 2 : (k + 1) * D // 2],
                (((1,), (1,)), ((), ())),
                preferred_element_type=F32,
            )
            for i in range(4)
        ]
        term = jnp.concatenate(terms, axis=1)
        hidden = term if k == 0 else hidden + term
    activated = jax.nn.gelu(hidden).astype(BF16)
    for z in range(SIDE):
        base = z * SHARE * LANES
        columns = second_ref[0, :, base : base + SHARE * LANES]
        store_share(out_ref, z, jnp.dot(activated, columns, preferred_element_type=F32))


def mix_kernel(in_ref, combine_ref, out_ref, mixed_ref, sems):
    copies = []
    for z in range(SIDE):
        columns = slice(z * SHARE * LANES, (z + 1) * SHARE * LANES)
        mixed_ref[:, columns] = jnp.dot(
            combine_ref[...], load_share(in_ref, z), preferred_element_type=F32
        ).astype(BF16)
        copy = pltpu.make_async_copy(mixed_ref.at[:, columns], out_ref.at[0, :, columns], sems.at[z])
        copy.start()
        copies.append(copy)
    for copy in copies:
        copy.wait()


def exchange(x, axes, groups=None):
    return lax.all_to_all(x, axes, split_axis=0, concat_axis=0, tiled=True, axis_index_groups=groups)


def column(h, z):
    return (z + 2 * ((h + 1) // 2 % 2)) % SIDE


NEAR = [sorted((SIDE * h + z for z in range(SIDE)), key=lambda p: column(p // SIDE, p % SIDE)) for h in range(SIDE)]
FAR = [[near[z] for near in NEAR] for z in range(SIDE)]


def near_cores(x):
    groups = [[CORES * z + c for z in near for c in range(CORES)] for near in NEAR]
    return exchange(x, ("zh", "zl", "core"), groups)


def far(x, axis):
    groups = [[SIDE * z + g for g in range(SIDE) for z in far] for far in FAR]
    return exchange(x, ("zh", "zl", axis), groups)


def near(x, axis):
    groups = [[SIDE * z + g for g in range(SIDE) for z in near] for near in NEAR]
    return exchange(x, ("zh", "zl", axis), groups)


def shards(patches, slot_keys, w_in, w_out):
    rows = patches.shape[1]
    tall = sds((CORES * SIDE, TALL, LANES), BF16)
    tall_stats = sds((CORES * SIDE, TALL + 8, LANES), BF16)
    wide = sds((PEERS, WIDE, LANES), BF16)
    flat_stats = sds((PEERS, 4, FLAT), BF16)

    own_key = call(
        key_kernel,
        sds((EXP, BLOCKS, LANES), BF16),
        [VMEM, ANY],
        [pltpu.VMEM((BLOCKS, LANES), F32)],
    )(slot_keys, pltpu.with_memory_space_constraint(patches, pltpu.HBM))
    keys = exchange(own_key, ("x", "y", "core"))
    terms, combine = call(
        dispatch_kernel,
        (tall_stats, sds((rows, EXP), BF16)),
        [VMEM, VMEM],
        [pltpu.VMEM((EXP * BLOCKS, LANES), F32), pltpu.VMEM((EXP, D), BF16)],
    )(patches, keys)

    spread = [pltpu.VMEM((32 * SHARE, LANES), F32)]
    parts = call(merge_near_kernel, flat_stats, [VMEM])(near_cores(terms))
    slot_tiles = call(merge_far_kernel, wide, [VMEM], spread)(far(parts, "x"))
    out_terms = call(ffn_kernel, tall, [VMEM] * 3)(
        near(slot_tiles, "y"), jnp.swapaxes(w_in, 1, 2), w_out
    )
    parts = call(add_near_kernel, wide, [VMEM])(near_cores(out_terms))
    out_tiles = call(add_far_kernel, wide, [VMEM], spread)(far(parts, "y"))
    return call(
        mix_kernel,
        sds((1, rows, D), BF16),
        [VMEM, VMEM],
        [pltpu.VMEM((rows, D), BF16), pltpu.SemaphoreType.DMA((SIDE,))],
        out_specs=ANY,
    )(near(out_tiles, "x"), combine)


def solution(mesh):
    split = Mesh(
        mesh.devices.reshape(SIDE, SIDE, SIDE, SIDE, CORES), ("zh", "zl", "x", "y", "core")
    )
    seq, exp = ("zh", "zl"), ("x", "y", "core")
    placed = (P(exp, seq, None), P(exp, None), P(exp, None, seq), P(exp, seq, None))
    return jax.shard_map(
        shards, mesh=split, in_specs=placed, out_specs=P(exp, seq, None), check_vma=False
    )
```
